128 devices in a mesh: mod: 4 (over y_lo, core), dp: 16 (over x, z), tp: 2 (over y_hi).
Axes of the slice: x: 4, y: 4 (y_hi: 2, y_lo: 2; y = y_hi * 2 + y_lo), z: 4, core: 2. Of those that a mesh axis runs over, the one named last changes fastest.
Arguments:
- tokens: bfloat16 [128, 257, 1280], P(('mod', 'dp')), may hold values from -133 to 133
- w_qkv: bfloat16 [1280, 3, 1280], P('mod', None, 'tp'), may hold values from -0.15625 to 0.15625
- w_out: bfloat16 [1280, 1280], P('mod', 'tp'), may hold values from -0.15625 to 0.15625
- w_proj: bfloat16 [1280, 1024], P('mod'), may hold values from -0.15625 to 0.15625
- other_emb: bfloat16 [128, 1024], P(('mod', 'dp')), may hold values from -6 to 6
Outputs:
- loss: float32 [4], P('mod')
- grad_tokens: bfloat16 [128, 257, 1280], P(('mod', 'dp'), None, 'tp')
- grad_qkv: float32 [1280, 3, 1280], P(('mod', 'dp'), None, 'tp')
- grad_out: float32 [1280, 1280], P(('mod', 'dp'), 'tp')
- grad_proj: float32 [1280, 1024], P(('mod', 'dp'))
- grad_other: bfloat16 [128, 1024], P(('mod', 'dp'))
The draws below stay inside these ranges and needn't reach their ends.
All inputs are finite; a program needn't handle non-finite values.
Results may differ from the reference program's by a relative error of at most 0.02.
Values may be sent and summed in bfloat16 or wider, within the bound.
A program may use at most 128 MiB of HBM per device.

```python
import jax
import jax.numpy as jnp
from jax import lax

D = 1280
HEADS = 16
HEAD_DIM = 80
E = 1024
TOK = 257
IMG_DEV = 2
PAIRS = 32
BATCH = 128
N_MOD = 4


def draw_tokens(key, part):
    key = jax.random.fold_in(key, 11)
    key_base, key_spread, key_rows = jax.random.split(key, 3)
    shape_all = (BATCH, TOK, D)
    base = jnp.clip(jax.random.normal(key_base, shape_all, jnp.float32), -4.0, 4.0)
    top_scale = 10.0
    spread = jnp.exp(jax.random.uniform(key_spread, shape_all, jnp.float32, -1.2, 1.2))
    row_scale = jnp.exp(jax.random.uniform(key_rows, (BATCH, TOK, 1), jnp.float32, 0.0, jnp.log(top_scale)))
    first_token = (jnp.arange(TOK) == 0)[None, :, None]
    row_scale = jnp.where(first_token, 1.0, row_scale)
    return (base * spread * row_scale).astype(jnp.bfloat16)


def block_scale(stream_key, dims, pieces, least, largest):
    level, own = 1.0, jax.random.fold_in(stream_key, 6)
    for position, blocks in pieces:
        heights = jnp.exp(jax.random.uniform(jax.random.fold_in(own, position), (blocks,), jnp.float32, least / len(pieces), largest / len(pieces)))
        level = level * jnp.repeat(heights, dims[position] // blocks).reshape([-1 if axis == position else 1 for axis in range(len(dims))])
    return level


def bell_draw(rng, extent, deviation, limit, pieces=(), kind=jnp.bfloat16):
    loudness = block_scale(rng, extent, pieces, -0.22, 0.18) if pieces else 1.0
    result = jax.random.normal(rng, extent, jnp.float32) * deviation * loudness
    return jnp.minimum(jnp.maximum(result, -limit), limit).astype(kind)


def setup_inputs(seed: int = 0) -> dict:
    key_of = jax.random.split(jax.random.key(seed), 6)
    tokens = draw_tokens(jax.random.fold_in(key_of[5], 71), 0)
    w_qkv = bell_draw(key_of[1], (D, 3, D), D ** -0.5, 0.15625, ((0, 4), (2, 2)))
    w_out = bell_draw(key_of[2], (D, D), D ** -0.5, 0.15625, ((0, 4), (1, 2)))
    w_proj = bell_draw(key_of[3], (D, E), D ** -0.5, 0.15625, ((0, 4),))
    other_emb = bell_draw(key_of[4], (BATCH, E), 1.0, 6.0, ((0, 64),))
    return dict(tokens=tokens, w_qkv=w_qkv, w_out=w_out, w_proj=w_proj, other_emb=other_emb)


EPSILON = 1e-06
LOGIT_SCALE = 1.0 / 0.07

def layer_stats(values):
    centered = values - lax.optimization_barrier(jnp.mean(values, axis=-1, keepdims=True))
    inv_std = lax.rsqrt(lax.optimization_barrier(jnp.mean(centered * centered, axis=-1, keepdims=True)) + EPSILON)
    return (centered * inv_std, inv_std)

def layer_back(grad_in, normed, inv_std):
    mean_grad = lax.optimization_barrier(jnp.mean(grad_in, axis=-1, keepdims=True))
    mean_cross = lax.optimization_barrier(jnp.mean(grad_in * normed, axis=-1, keepdims=True))
    return inv_std * (grad_in - mean_grad - normed * mean_cross)

def attention_parts(block, w_qkv):
    rows_n = block.shape[0]
    normed, inv_std = layer_stats(block.astype(jnp.float32))
    normed_b = normed.astype(jnp.bfloat16)
    flat_rows = normed_b.reshape(rows_n * TOK, D)
    kv_weight = w_qkv[:, 1:3, :].reshape(D, 2 * D)
    key_value = jnp.dot(flat_rows, kv_weight, preferred_element_type=jnp.float32).astype(jnp.bfloat16)
    key_rows = key_value[:, :D].reshape(rows_n, TOK, HEADS, HEAD_DIM)
    value_rows = key_value[:, D:].reshape(rows_n, TOK, HEADS, HEAD_DIM)
    query_b = jnp.dot(normed_b[:, 0], w_qkv[:, 0, :], preferred_element_type=jnp.float32).astype(jnp.bfloat16)
    query_heads = query_b.reshape(rows_n, HEADS, HEAD_DIM).astype(jnp.float32)
    scale_dot = HEAD_DIM ** (-0.5)
    scores = jnp.einsum('nhd,nthd->nht', query_heads, key_rows.astype(jnp.float32)) * scale_dot
    expo = jnp.exp(scores)
    soft = expo / lax.optimization_barrier(jnp.sum(expo, axis=-1, keepdims=True))
    soft_b = soft.astype(jnp.bfloat16)
    context = jnp.einsum('nht,nthd->nhd', soft_b.astype(jnp.float32), value_rows.astype(jnp.float32))
    context_b = context.astype(jnp.bfloat16).reshape(rows_n, D)
    return (normed, inv_std, normed_b, flat_rows, key_rows, value_rows, query_heads, soft, soft_b, context_b)

def reference(tokens, w_qkv, w_out, w_proj, other_emb):
    blocks = tokens.reshape(BATCH // IMG_DEV, IMG_DEV, TOK, D)

    def forward_block(block):
        parts = attention_parts(block, w_qkv)
        context_b = parts[9]
        attn = jnp.dot(context_b, w_out.T, preferred_element_type=jnp.float32)
        return (block[:, 0].astype(jnp.float32) + attn, context_b)
    hidden_blocks, context_blocks = lax.map(forward_block, blocks)
    hidden_row = hidden_blocks.reshape(BATCH, D)
    context_b = context_blocks.reshape(BATCH, D)
    head_normed, head_inv = layer_stats(hidden_row)
    head_b = head_normed.astype(jnp.bfloat16)
    proj_rows = jnp.dot(head_b, w_proj, preferred_element_type=jnp.float32)
    proj_inv = lax.rsqrt(lax.optimization_barrier(jnp.sum(proj_rows * proj_rows, axis=-1, keepdims=True)) + EPSILON)
    embed = proj_rows * proj_inv
    embed_b = embed.astype(jnp.bfloat16)
    other_f = other_emb.astype(jnp.float32)
    other_inv = lax.rsqrt(lax.optimization_barrier(jnp.sum(other_f * other_f, axis=-1, keepdims=True)) + EPSILON)
    other_unit = other_f * other_inv
    other_b = other_unit.astype(jnp.bfloat16)
    embed_groups = embed_b.reshape(N_MOD, PAIRS, E).astype(jnp.float32)
    other_groups = other_b.reshape(N_MOD, PAIRS, E).astype(jnp.float32)
    logits = LOGIT_SCALE * jnp.einsum('mie,mje->mij', embed_groups, other_groups)
    expo = jnp.exp(logits)
    row_total = lax.optimization_barrier(jnp.sum(expo, axis=2))
    col_total = lax.optimization_barrier(jnp.sum(expo, axis=1))
    diag_vals = jnp.diagonal(logits, axis1=1, axis2=2)
    loss = (0.5 * lax.optimization_barrier(jnp.sum(jnp.log(row_total), axis=1)) + 0.5 * lax.optimization_barrier(jnp.sum(jnp.log(col_total), axis=1)) - lax.optimization_barrier(jnp.sum(diag_vals, axis=1))) / PAIRS
    identity = jnp.eye(PAIRS, dtype=jnp.float32)[None]
    grad_logit = 0.5 / PAIRS * (expo / row_total[:, :, None] + expo / col_total[:, None, :]) - identity / PAIRS
    grad_logit_b = grad_logit.astype(jnp.bfloat16).astype(jnp.float32)
    d_embed = (LOGIT_SCALE * jnp.einsum('mij,mje->mie', grad_logit_b, other_groups)).reshape(BATCH, E)
    d_unit = (LOGIT_SCALE * jnp.einsum('mij,mie->mje', grad_logit_b, embed_groups)).reshape(BATCH, E)
    d_proj = (d_embed - embed * lax.optimization_barrier(jnp.sum(embed * d_embed, axis=-1, keepdims=True))) * proj_inv
    d_proj_b = d_proj.astype(jnp.bfloat16)
    grad_other = ((d_unit - other_unit * lax.optimization_barrier(jnp.sum(other_unit * d_unit, axis=-1, keepdims=True))) * other_inv).astype(jnp.bfloat16)
    d_head = jnp.dot(d_proj_b, w_proj.T, preferred_element_type=jnp.float32)
    d_hidden = layer_back(d_head, head_normed, head_inv)
    d_hidden_b = d_hidden.astype(jnp.bfloat16)
    grad_proj = jnp.dot(head_b.T, d_proj_b, preferred_element_type=jnp.float32)
    grad_out = jnp.dot(d_hidden_b.T, context_b, preferred_element_type=jnp.float32)
    kv_weight = w_qkv[:, 1:3, :].reshape(D, 2 * D)
    scale_dot = HEAD_DIM ** (-0.5)

    def backward_block(carry, inputs):
        block, hidden_grad_b, hidden_grad = inputs
        rows_n = block.shape[0]
        normed, inv_std, normed_b, flat_rows, key_rows, value_rows, query_heads, soft, soft_b, ctx_unused = attention_parts(block, w_qkv)
        d_context = jnp.dot(hidden_grad_b, w_out, preferred_element_type=jnp.float32)
        d_context_b = d_context.astype(jnp.bfloat16).reshape(rows_n, HEADS, HEAD_DIM).astype(jnp.float32)
        d_soft = jnp.einsum('nhd,nthd->nht', d_context_b, value_rows.astype(jnp.float32))
        d_score = soft * (d_soft - lax.optimization_barrier(jnp.sum(soft * d_soft, axis=-1, keepdims=True)))
        d_score_b = d_score.astype(jnp.bfloat16).astype(jnp.float32)
        d_query = jnp.einsum('nht,nthd->nhd', d_score_b, key_rows.astype(jnp.float32)) * scale_dot
        d_query_b = d_query.astype(jnp.bfloat16).reshape(rows_n, D)
        d_key = jnp.einsum('nht,nhd->nthd', d_score, query_heads) * scale_dot
        d_value = jnp.einsum('nht,nhd->nthd', soft_b.astype(jnp.float32), d_context_b)
        kv_grad_b = jnp.concatenate([d_key.reshape(rows_n * TOK, D), d_value.reshape(rows_n * TOK, D)], axis=1).astype(jnp.bfloat16)
        d_normed = jnp.dot(kv_grad_b, kv_weight.T, preferred_element_type=jnp.float32).reshape(rows_n, TOK, D)
        d_normed = d_normed.at[:, 0].add(jnp.dot(d_query_b, w_qkv[:, 0, :].T, preferred_element_type=jnp.float32))
        d_tokens = layer_back(d_normed, normed, inv_std)
        d_tokens = d_tokens.at[:, 0].add(hidden_grad).astype(jnp.bfloat16)
        grad_query = jnp.dot(normed_b[:, 0].T, d_query_b, preferred_element_type=jnp.float32)
        grad_kv = jnp.dot(flat_rows.T, kv_grad_b, preferred_element_type=jnp.float32).reshape(D, 2, D)
        carry = carry + jnp.concatenate([grad_query[:, None, :], grad_kv], axis=1)
        return (carry, d_tokens)
    start_grad = jnp.zeros((D, 3, D), jnp.float32)
    grad_qkv, token_blocks = lax.scan(backward_block, start_grad, (blocks, d_hidden_b.reshape(BATCH // IMG_DEV, IMG_DEV, D), d_hidden.reshape(BATCH // IMG_DEV, IMG_DEV, D)))
    grad_tokens = token_blocks.reshape(BATCH, TOK, D)
    return (loss, grad_tokens, grad_qkv, grad_out, grad_proj, grad_other)
```

```python
import functools

import jax
import jax.numpy as jnp
from jax import lax
from jax.experimental import pallas as pl
from jax.experimental.pallas import tpu as pltpu
from jax.sharding import PartitionSpec as P

HEAD_DIM = 80
EPSILON = 1e-06
LOGIT_SCALE = 1.0 / 0.07
MESH = pl.DeviceIdType.MESH
F32 = jnp.float32
BF16 = jnp.bfloat16

N_MOD, N_DP, N_TP = 4, 16, 2
IMGS = 2
GROUP = N_MOD * IMGS
HEADS = 8
TOK = 257
ROWS = IMGS * TOK
PAD_ROWS = 528
CHUNK = 176
D = 1280
HALF = D // 2
SLICE = D // N_MOD
OUT_ROWS = SLICE // N_DP
E = 1024
PAIRS = 32
ALL = GROUP * N_DP
SCALE = HEAD_DIM**-0.5


def dot(a, b):
    return jnp.dot(a, b, preferred_element_type=F32)


def dot_nt(a, b):
    return lax.dot_general(a, b, (((1,), (1,)), ((), ())), preferred_element_type=F32)


def dot_tn(a, b):
    return lax.dot_general(a, b, (((0,), (0,)), ((), ())), preferred_element_type=F32)


def split_high_low(v):
    high = v.astype(BF16)
    low = (v - high.astype(F32)).astype(BF16)
    return jnp.concatenate([high.astype(F32), low.astype(F32)], axis=0).astype(BF16)


def fold_halves(v):
    k = v.shape[1] // 2
    return jnp.concatenate([v[:, :k], v[:, k:]], axis=0).astype(BF16)


def unfold_halves(v):
    wide = v.astype(F32)
    return jnp.concatenate(
        [wide[:, :8].reshape(ALL, -1), wide[:, 8:].reshape(ALL, -1)], axis=1
    )


def head_mask():
    lane = lax.broadcasted_iota(jnp.int32, (HEADS, HALF), 1)
    head = lax.broadcasted_iota(jnp.int32, (HEADS, HALF), 0) * HEAD_DIM
    return (lane >= head) & (lane < head + HEAD_DIM)


def expand_heads(v, mask):
    return jnp.concatenate(
        [jnp.where(mask, v[b : b + 1], 0.0) for b in range(GROUP)], axis=0
    ).astype(BF16)


def collapse_heads(v, mask):
    return jnp.concatenate(
        [
            jnp.sum(
                jnp.where(mask, v[b * HEADS : (b + 1) * HEADS], 0.0), axis=0, keepdims=True
            )
            for b in range(GROUP)
        ],
        axis=0,
    )


def row_sum(v):
    return jnp.sum(v, axis=-1, keepdims=True)


def kernel(
    x_ref, wqkv_ref, wout_ref, wproj_ref, other_ref,
    loss_ref, gtok_ref, gqkv_ref, gout_ref, gproj_ref, gother_ref,
    xn_ref, mu_ref, inv_ref, grad_ref, dn_ref, dn0_ref, unit_ref, qbd_ref, dbd_ref,
    s_cls, d_cls, s_oth, d_oth, s_q, d_q, s_kq, d_kq, s_w, d_w, s_ctx, d_ctx, s_att, d_att,
    s_prj, d_prj, s_hs, d_hs, s_dh, d_dh, s_vd, d_vd, s_u, d_u, s_dq, d_dq, s_cg, d_cg,
    s_sc, d_sc, s_kv, d_kv,
    f_oth, g_oth, f_emb, g_emb, f_dpr, g_dpr, f_qc, g_qc, f_dd, g_dd, f_ea, g_ea, f_la, g_la,
    mod_send, mod_recv, all_send, all_recv, tp_send, tp_recv, dp_send, dp_recv,
):
    m, d, t = lax.axis_index("mod"), lax.axis_index("dp"), lax.axis_index("tp")
    me = t * N_MOD + m

    barrier = pltpu.get_barrier_semaphore()
    for k in range(1, N_MOD):
        pl.semaphore_signal(
            barrier, 1, device_id=(lax.rem(m + k, N_MOD), d, t), device_id_type=MESH
        )
    for k in range(N_MOD):
        pl.semaphore_signal(
            barrier, 1, device_id=(lax.rem(m + k, N_MOD), d, 1 - t), device_id_type=MESH
        )

    def greet(k, carry):
        pl.semaphore_signal(
            barrier, 1, device_id=(m, lax.rem(d + k, N_DP), t), device_id_type=MESH
        )
        return carry

    lax.fori_loop(1, N_DP, greet, 0)

    def mod_copy(n, k, src, dst, slot):
        peer = lax.rem(m + k, N_MOD)
        return pltpu.make_async_remote_copy(
            src(peer),
            dst.at[m if slot is None else peer],
            mod_send.at[n, k],
            mod_recv.at[n, m if slot is None else peer],
            device_id=(peer, d, t),
            device_id_type=MESH,
        )

    def mod_start(n, src, dst):
        for k in range(1, N_MOD):
            mod_copy(n, k, src, dst, None).start()

    def mod_wait(n, src, dst):
        for k in range(1, N_MOD):
            mod_copy(n, k, src, dst, 0).wait_recv()

    def mod_end(n, src, dst):
        for k in range(1, N_MOD):
            mod_copy(n, k, src, dst, None).wait_send()

    def all_copy(n, k, src, dst, landing):
        peer_m = lax.rem(m + k, N_MOD)
        peer_t = t if k < N_MOD else 1 - t
        slot = peer_t * N_MOD + peer_m if landing else me
        return pltpu.make_async_remote_copy(
            src,
            dst.at[slot],
            all_send.at[n, k],
            all_recv.at[n, slot],
            device_id=(peer_m, d, peer_t),
            device_id_type=MESH,
        )

    def all_start(n, src, dst):
        for k in range(1, 2 * N_MOD):
            all_copy(n, k, src, dst, False).start()

    def all_wait(n, src, dst):
        for k in range(1, 2 * N_MOD):
            all_copy(n, k, src, dst, True).wait_recv()

    def all_end(n, src, dst):
        for k in range(1, 2 * N_MOD):
            all_copy(n, k, src, dst, False).wait_send()

    def dp_copy(n, k, src, dst, landing):
        peer = lax.rem(d + k, N_DP)
        slot = peer if landing else d
        return pltpu.make_async_remote_copy(
            src(peer),
            dst.at[slot],
            dp_send.at[n, k],
            dp_recv.at[n, slot],
            device_id=(m, peer, t),
            device_id_type=MESH,
        )

    def dp_start(n, src, dst):
        def body(k, carry):
            dp_copy(n, k, src, dst, False).start()
            return carry

        lax.fori_loop(1, N_DP, body, 0)

    def dp_wait(n, src, dst):
        def body(k, carry):
            dp_copy(n, k, src, dst, True).wait_recv()
            return carry

        lax.fori_loop(1, N_DP, body, 0)

    def dp_end(n, src, dst):
        def body(k, carry):
            dp_copy(n, k, src, dst, False).wait_send()
            return carry

        lax.fori_loop(1, N_DP, body, 0)

    def tp_copy(n, src, dst):
        return pltpu.make_async_remote_copy(
            src, dst, tp_send.at[n], tp_recv.at[n], device_id=(m, d, 1 - t), device_id_type=MESH
        )

    def whole(ref):
        return lambda peer: ref

    def part(ref):
        return lambda peer: ref.at[peer]

    row8 = lax.broadcasted_iota(jnp.int32, (GROUP, 1), 0)
    mask = head_mask()

    def place(v):
        return jnp.where(row8 == 2 * m, v[0:1], jnp.where(row8 == 2 * m + 1, v[1:2], 0.0))

    def own_rows(v):
        first = jnp.sum(jnp.where(row8 == 2 * m, v, 0.0), axis=0, keepdims=True)
        second = jnp.sum(jnp.where(row8 == 2 * m + 1, v, 0.0), axis=0, keepdims=True)
        return jnp.where(row8 == 0, first, jnp.where(row8 == 1, second, 0.0))

    def normalise(c):
        at = pl.ds(c * CHUNK, CHUNK)
        x = x_ref[at, :].astype(F32)
        mu = row_sum(x) * (1.0 / D)
        x = x - mu
        inv = lax.rsqrt(row_sum(x * x) * (1.0 / D) + EPSILON)
        xn_ref[at, :] = (x * inv).astype(BF16)
        mu_ref[at, :] = mu
        inv_ref[at, :] = inv

    def windows(dst, v):
        wide = jnp.concatenate([v, jnp.zeros((v.shape[0], 192), F32)], axis=1)
        for k in range(N_DP):
            dst[k] = wide[:, k * OUT_ROWS : k * OUT_ROWS + 128].astype(BF16)

    x8 = x_ref[0:16, :].astype(F32)[0:8]
    mu8 = row_sum(x8) * (1.0 / D)
    c8 = x8 - mu8
    n8 = c8 * lax.rsqrt(row_sum(c8 * c8) * (1.0 / D) + EPSILON)
    cls = jnp.concatenate([place(n8), place(x8)], axis=0)
    for p in range(N_MOD):
        s_cls[p] = cls[:, p * SLICE : (p + 1) * SLICE]
    d_cls[m] = s_cls[m]
    oth = place(other_ref[...].astype(F32))
    s_oth[...] = oth
    d_oth[m] = oth
    pl.semaphore_wait(barrier, N_MOD - 1 + N_MOD + N_DP - 1)
    mod_start(0, part(s_cls), d_cls)
    mod_start(1, whole(s_oth), d_oth)
    normalise(0)
    mod_wait(0, part(s_cls), d_cls)
    cls = d_cls[0] + d_cls[1] + d_cls[2] + d_cls[3]
    n0, x0 = cls[0:8], cls[8:16]

    qp = dot(n0.astype(BF16), wqkv_ref[0])
    s_q[...] = qp
    d_q[m] = qp
    mod_start(2, whole(s_q), d_q)
    normalise(1)
    mod_wait(1, whole(s_oth), d_oth)
    oth = fold_halves(d_oth[0] + d_oth[1] + d_oth[2] + d_oth[3])
    f_oth[...] = oth
    g_oth[d] = oth
    mod_wait(2, whole(s_q), d_q)
    q = (d_q[0] + d_q[1] + d_q[2] + d_q[3]).astype(BF16).astype(F32)

    kq = dot_nt(expand_heads(q, mask), wqkv_ref[1])
    for p in range(N_MOD):
        s_kq[p] = kq[p * 16 : (p + 1) * 16]
    d_kq[m] = s_kq[m]
    mod_start(3, part(s_kq), d_kq)
    dp_start(0, whole(f_oth), g_oth)
    normalise(2)
    mod_wait(3, part(s_kq), d_kq)
    kq_b = jnp.concatenate([d_kq[p] for p in range(N_MOD)], axis=1).astype(BF16)

    scores = dot_nt(kq_b, xn_ref[...]) * SCALE
    lane = lax.broadcasted_iota(jnp.int32, (16, PAD_ROWS), 1)
    image = lax.broadcasted_iota(jnp.int32, (16, PAD_ROWS), 0) >= HEADS
    valid = (((lane & 1) == 1) == image) & (lane < ROWS)
    expo = jnp.where(valid, jnp.exp(scores), 0.0)
    soft = expo / row_sum(expo)
    soft_b = soft.astype(BF16)
    w = dot(soft_b, xn_ref[...])
    for p in range(N_MOD):
        s_w[p] = w[:, p * SLICE : (p + 1) * SLICE]
    d_w[m] = s_w[m]
    mod_start(4, part(s_w), d_w)
    mod_wait(4, part(s_w), d_w)
    w64 = d_w[...].reshape(64, SLICE)

    cp = collapse_heads(dot(w64.astype(BF16), wqkv_ref[2]), mask)
    s_ctx[...] = cp
    d_ctx[m] = cp
    mod_start(5, whole(s_ctx), d_ctx)
    windows(f_ea, jnp.concatenate([w64, n0, n0], axis=0))
    g_ea[d] = f_ea[d]
    dp_start(1, part(f_ea), g_ea)
    mod_wait(5, whole(s_ctx), d_ctx)
    ctx = d_ctx[0] + d_ctx[1] + d_ctx[2] + d_ctx[3]

    ap = dot_nt(ctx.astype(BF16), wout_ref[...]) + jnp.where(t == 0, x0, 0.0)
    s_att[...] = ap
    d_att[me] = ap
    all_start(0, s_att, d_att)
    qc = jnp.concatenate([q, ctx], axis=0).astype(BF16)
    f_qc[...] = qc
    g_qc[d] = qc
    dp_start(2, whole(f_qc), g_qc)
    all_wait(0, s_att, d_att)
    hid = [d_att[p] + d_att[p + N_MOD] for p in range(N_MOD)]
    hmu = sum(row_sum(h) for h in hid) * (1.0 / D)
    hvar = sum(row_sum((h - hmu) * (h - hmu)) for h in hid) * (1.0 / D)
    hinv = lax.rsqrt(hvar + EPSILON)
    hn = (d_att[m] + d_att[m + N_MOD] - hmu) * hinv

    pp = dot(hn.astype(BF16), wproj_ref[...])
    s_prj[...] = pp
    d_prj[m] = pp
    mod_start(6, whole(s_prj), d_prj)
    hs = dot(
        jnp.concatenate([split_high_low(hn), jnp.ones((16, SLICE), BF16)], axis=0), wout_ref[...]
    )
    hs = jnp.concatenate([hs[0:8] + hs[8:16], hs[16:24]], axis=0)
    s_hs[...] = hs
    d_hs[m] = hs
    mod_start(7, whole(s_hs), d_hs)
    dp_wait(0, whole(f_oth), g_oth)
    other_f = unfold_halves(g_oth[...])
    other_inv = lax.rsqrt(row_sum(other_f * other_f) + EPSILON)
    unit = other_f * other_inv
    unit_ref[...] = unit
    unit_b = unit.astype(BF16)
    mod_wait(6, whole(s_prj), d_prj)
    proj = d_prj[0] + d_prj[1] + d_prj[2] + d_prj[3]
    pinv = lax.rsqrt(row_sum(proj * proj) + EPSILON)
    embed = proj * pinv
    emb = fold_halves(embed)
    f_emb[...] = emb
    g_emb[d] = emb
    dp_start(3, whole(f_emb), g_emb)

    def spread(k, carry):
        v = g_qc[k].astype(F32)
        qbd_ref[pl.ds(k * 64, 64), :] = expand_heads(v[0:8], mask)
        return carry

    dp_wait(2, whole(f_qc), g_qc)
    lax.fori_loop(0, N_DP, spread, 0)
    dp_wait(3, whole(f_emb), g_emb)

    emb_b = unfold_halves(g_emb[...]).astype(BF16)
    logits = dot_nt(emb_b, unit_b) * LOGIT_SCALE
    left = lax.broadcasted_iota(jnp.int32, (ALL, ALL), 0)
    right = lax.broadcasted_iota(jnp.int32, (ALL, ALL), 1)
    paired = ((left >> 1) & 3) == ((right >> 1) & 3)
    ex = jnp.where(paired, jnp.exp(logits), 0.0)
    row_total = row_sum(ex)
    col_total = jnp.sum(ex, axis=0, keepdims=True)
    grad = (0.5 / PAIRS) * (ex / row_total + ex / col_total)
    grad = grad - jnp.where(left == right, 1.0 / PAIRS, 0.0)
    grad_ref[...] = grad
    grad8 = grad_ref[pl.ds(d * GROUP, GROUP), :].astype(BF16)
    d_embed = LOGIT_SCALE * dot(grad8, unit_b)
    d_proj = (d_embed - embed * row_sum(embed * d_embed)) * pinv
    d_proj_b = d_proj.astype(BF16)
    dh = dot_nt(d_proj_b, wproj_ref[...])
    da = dot(split_high_low(dh), wout_ref[...])
    lane = lax.broadcasted_iota(jnp.int32, (GROUP, 128), 1)
    stats = jnp.where(lane == 0, row_sum(dh), jnp.where(lane == 1, row_sum(dh * hn), 0.0))
    da = jnp.concatenate([da[0:8] + da[8:16], stats], axis=1)
    s_dh[...] = da
    d_dh[m] = da
    mod_start(8, whole(s_dh), d_dh)
    dpr = fold_halves(d_proj)
    f_dpr[...] = dpr
    g_dpr[d] = dpr
    dp_start(4, whole(f_dpr), g_dpr)

    rows_m = ((lax.broadcasted_iota(jnp.int32, (ALL, 1), 0) >> 1) & 3) == m
    cols_m = ((lax.broadcasted_iota(jnp.int32, (1, ALL), 1) >> 1) & 3) == m
    diag = row_sum(jnp.where(left == right, logits, 0.0))
    loss = jnp.sum(
        jnp.where(rows_m, 0.5 * jnp.log(row_total) - diag, 0.0), axis=0, keepdims=True
    ) + row_sum(jnp.where(cols_m, 0.5 * jnp.log(col_total), 0.0))
    loss_ref[...] = jnp.broadcast_to(loss * (1.0 / PAIRS), (8, 128))
    d_unit = LOGIT_SCALE * dot_tn(grad.astype(BF16), emb_b)
    grad_other = (d_unit - unit * row_sum(unit * d_unit)) * other_inv
    unit_ref[...] = grad_other
    gother_ref[...] = own_rows(unit_ref[pl.ds(d * GROUP, GROUP), :])

    mod_wait(7, whole(s_hs), d_hs)
    hs = d_hs[0] + d_hs[1] + d_hs[2] + d_hs[3]
    mod_wait(8, whole(s_dh), d_dh)
    da = d_dh[0] + d_dh[1] + d_dh[2] + d_dh[3]
    m1 = da[:, HALF : HALF + 1] * (1.0 / D)
    m2 = da[:, HALF + 1 : HALF + 2] * (1.0 / D)
    d_context = hinv * (da[:, :HALF] - m1 * hs[8:16] - m2 * hs[0:8])
    d_hidden = hinv * (dh - m1 - hn * m2)

    vd = dot_nt(expand_heads(d_context, mask), wqkv_ref[2])
    for p in range(N_MOD):
        s_vd[p] = jnp.concatenate([vd[p * 16 : (p + 1) * 16], d_hidden], axis=0)
    d_vd[m] = s_vd[m]
    mod_start(9, part(s_vd), d_vd)
    mod_wait(9, part(s_vd), d_vd)
    vd_b = jnp.concatenate([d_vd[p, 0:16] for p in range(N_MOD)], axis=1).astype(BF16)
    d_soft = dot_nt(vd_b, xn_ref[...])
    d_score = soft * (d_soft - row_sum(soft * d_soft))
    d_score_b = d_score.astype(BF16)
    u = dot(d_score_b, xn_ref[...]) * SCALE
    for p in range(N_MOD):
        s_u[p] = u[:, p * SLICE : (p + 1) * SLICE]
    d_u[m] = s_u[m]
    mod_start(10, part(s_u), d_u)
    s_sc[0:16] = (d_score * SCALE).astype(BF16)
    s_sc[16:32] = soft_b
    s_kv[0:16] = kq_b
    s_kv[16:32] = vd_b
    tp_copy(0, s_sc, d_sc).start()
    tp_copy(1, s_kv, d_kv).start()
    mod_wait(10, part(s_u), d_u)
    u64 = d_u[...].reshape(64, SLICE)
    dqp = collapse_heads(dot(u64.astype(BF16), wqkv_ref[1]), mask)
    s_dq[...] = dqp
    d_dq[m] = dqp
    mod_start(11, whole(s_dq), d_dq)
    windows(f_la, jnp.concatenate([u64, hn, d_hidden], axis=0))
    g_la[d] = f_la[d]
    dp_start(5, part(f_la), g_la)
    mod_wait(11, whole(s_dq), d_dq)
    dq = d_dq[0] + d_dq[1] + d_dq[2] + d_dq[3]
    dd = jnp.concatenate([dq, d_context], axis=0).astype(BF16)
    f_dd[...] = dd
    g_dd[d] = dd
    dp_start(6, whole(f_dd), g_dd)
    cg = dot_nt(dq.astype(BF16), wqkv_ref[0])
    s_cg[...] = cg
    d_cg[me] = cg
    all_start(1, s_cg, d_cg)

    tp_copy(0, s_sc, d_sc).wait_recv()
    tp_copy(1, s_kv, d_kv).wait_recv()
    weights = jnp.concatenate([s_sc[...], d_sc[...]], axis=0).astype(F32).T.astype(BF16)
    factors = jnp.concatenate([s_kv[...], d_kv[...]], axis=0)
    half = pl.ds(pl.multiple_of(t * HALF, 128), HALF)
    for c in range(PAD_ROWS // CHUNK):
        at = pl.ds(c * CHUNK, CHUNK)
        dn = dot(weights[c * CHUNK : (c + 1) * CHUNK], factors)
        mu, inv = mu_ref[at, :], inv_ref[at, :]
        xh = (x_ref[at, :].astype(F32) - mu) * inv
        mean_grad = row_sum(dn) * (1.0 / D)
        mean_cross = row_sum(dn * xh) * (1.0 / D)
        dn_ref[...] = dn
        if c == 0:
            dn0_ref[...] = dn[0:8]
        xh = (x_ref[at, half].astype(F32) - mu) * inv
        gtok_ref[at, :] = (inv * (dn_ref[:, half] - mean_grad - xh * mean_cross)).astype(BF16)

    all_wait(1, s_cg, d_cg)
    extra = own_rows(
        jnp.concatenate([d_cg[p] + d_cg[p + N_MOD] for p in range(N_MOD)], axis=1)
    )
    dn = dn0_ref[...] + extra
    mu, inv = mu_ref[0:8, :], inv_ref[0:8, :]
    xh = (x_ref[0:16, :].astype(F32)[0:8] - mu) * inv
    mean_grad = row_sum(dn) * (1.0 / D)
    mean_cross = row_sum(dn * xh) * (1.0 / D)
    dn0_ref[...] = inv * (dn - mean_grad - xh * mean_cross) + own_rows(
        jnp.concatenate([d_vd[p, 16:24] for p in range(N_MOD)], axis=1)
    )
    head_rows = gtok_ref[0:16, :].astype(F32)
    head_rows = jnp.concatenate(
        [jnp.where(row8 < 2, dn0_ref[:, half], head_rows[0:8]), head_rows[8:16]], axis=0
    )
    gtok_ref[0:16, :] = head_rows.astype(BF16)

    dp_wait(1, part(f_ea), g_ea)
    dp_wait(4, whole(f_dpr), g_dpr)
    dp_wait(5, part(f_la), g_la)
    la = g_la[...]
    gk = dot_tn(la[:, 0:64].reshape(1024, 128), qbd_ref[...])
    gqkv_ref[1] = gk[0:OUT_ROWS]
    tail = la[:, 64:80].astype(F32)
    hn_all = tail[:, 0:8].reshape(ALL, 128).astype(BF16)
    dhid_all = tail[:, 8:16].reshape(ALL, 128).astype(BF16)
    gproj_ref[...] = dot_tn(hn_all, unfold_halves(g_dpr[...]).astype(BF16))[0:OUT_ROWS]
    ctx_all = g_qc[...].astype(F32)[:, 8:16].reshape(ALL, HALF).astype(BF16)
    gout_ref[...] = dot_tn(dhid_all, ctx_all)[0:OUT_ROWS]
    dp_wait(6, whole(f_dd), g_dd)

    def spread_late(k, carry):
        v = g_dd[k].astype(F32)
        dbd_ref[pl.ds(k * 64, 64), :] = expand_heads(v[8:16], mask)
        return carry

    lax.fori_loop(0, N_DP, spread_late, 0)
    ea = g_ea[...]
    gv = dot_tn(ea[:, 0:64].reshape(1024, 128), dbd_ref[...])
    gqkv_ref[2] = gv[0:OUT_ROWS]
    n0_all = ea[:, 64:80].astype(F32)[:, 0:8].reshape(ALL, 128).astype(BF16)
    dq_all = g_dd[...].astype(F32)[:, 0:8].reshape(ALL, HALF).astype(BF16)
    gqkv_ref[0] = dot_tn(n0_all, dq_all)[0:OUT_ROWS]

    for n, src, dst in (
        (0, part(s_cls), d_cls), (1, whole(s_oth), d_oth), (2, whole(s_q), d_q),
        (3, part(s_kq), d_kq), (4, part(s_w), d_w), (5, whole(s_ctx), d_ctx),
        (6, whole(s_prj), d_prj), (7, whole(s_hs), d_hs), (8, whole(s_dh), d_dh),
        (9, part(s_vd), d_vd), (10, part(s_u), d_u), (11, whole(s_dq), d_dq),
    ):
        mod_end(n, src, dst)
    all_end(0, s_att, d_att)
    all_end(1, s_cg, d_cg)
    tp_copy(0, s_sc, d_sc).wait_send()
    tp_copy(1, s_kv, d_kv).wait_send()
    for n, src, dst in (
        (0, whole(f_oth), g_oth), (1, part(f_ea), g_ea), (2, whole(f_qc), g_qc),
        (3, whole(f_emb), g_emb), (4, whole(f_dpr), g_dpr), (5, part(f_la), g_la),
        (6, whole(f_dd), g_dd),
    ):
        dp_end(n, src, dst)


def local(tokens, w_qkv, w_out, w_proj, other_emb):
    rows = tokens.transpose(1, 0, 2).reshape(ROWS, D)
    rows = jnp.pad(rows, ((0, PAD_ROWS - ROWS), (0, 0)))
    vmem = pl.BlockSpec(memory_space=pltpu.VMEM)

    def pair(send, land, dtype=F32):
        return [pltpu.VMEM(send, dtype), pltpu.VMEM(land, dtype)]

    def mod_all(n, k):
        return pair((n, k), (N_MOD, n, k))

    def mod_each(n):
        return pair((N_MOD, n, SLICE), (N_MOD, n, SLICE))

    def dp_all(n, k):
        return pair((n, k), (N_DP, n, k), BF16)

    scratch = [
        pltpu.VMEM((PAD_ROWS, D), BF16),
        pltpu.VMEM((PAD_ROWS, 1), F32),
        pltpu.VMEM((PAD_ROWS, 1), F32),
        pltpu.VMEM((ALL, ALL), F32),
        pltpu.VMEM((CHUNK, D), F32),
        pltpu.VMEM((8, D), F32),
        pltpu.VMEM((ALL, E), F32),
        pltpu.VMEM((N_DP * 64, HALF), BF16),
        pltpu.VMEM((N_DP * 64, HALF), BF16),
    ]
    scratch += mod_each(16) + mod_all(8, E) + mod_all(8, HALF) + mod_each(16) + mod_each(16)
    scratch += mod_all(8, HALF) + pair((8, SLICE), (2 * N_MOD, 8, SLICE)) + mod_all(8, E)
    scratch += mod_all(16, HALF) + mod_all(8, HALF + 128) + mod_each(24) + mod_each(16)
    scratch += mod_all(8, HALF) + pair((8, SLICE), (2 * N_MOD, 8, SLICE))
    scratch += pair((32, PAD_ROWS), (32, PAD_ROWS), BF16) + pair((32, D), (32, D), BF16)
    scratch += dp_all(16, E // 2) + dp_all(16, E // 2) + dp_all(16, E // 2) + dp_all(16, HALF)
    scratch += dp_all(16, HALF) + pair((N_DP, 80, 128), (N_DP, 80, 128), BF16) * 2
    dma = pltpu.SemaphoreType.DMA
    scratch += [dma((12, N_MOD)), dma((12, N_MOD)), dma((2, 8)), dma((2, 8)), dma((2,)), dma((2,))]
    scratch += [dma((7, N_DP)), dma((7, N_DP))]
    loss, grad_rows, grad_qkv, grad_out, grad_proj, grad_other = pl.pallas_call(
        kernel,
        out_shape=[
            jax.ShapeDtypeStruct((8, 128), F32),
            jax.ShapeDtypeStruct((PAD_ROWS, HALF), BF16),
            jax.ShapeDtypeStruct((3, OUT_ROWS, HALF), F32),
            jax.ShapeDtypeStruct((OUT_ROWS, HALF), F32),
            jax.ShapeDtypeStruct((OUT_ROWS, E), F32),
            jax.ShapeDtypeStruct((8, E), F32),
        ],
        in_specs=[vmem] * 5,
        out_specs=[vmem] * 6,
        scratch_shapes=scratch,
        compiler_params=pltpu.CompilerParams(
            collective_id=0, has_side_effects=True, vmem_limit_bytes=48 * 2**20
        ),
    )(rows, w_qkv.transpose(1, 0, 2), w_out, w_proj, other_emb)
    grad_tokens = grad_rows[:ROWS].reshape(TOK, IMGS, HALF).transpose(1, 0, 2)
    return (
        loss[0, 0:1],
        grad_tokens,
        grad_qkv.transpose(1, 0, 2),
        grad_out,
        grad_proj,
        grad_other[0:IMGS].astype(BF16),
    )


def solution(mesh):
    placed = (
        P(("mod", "dp"), None, None),
        P("mod", None, "tp"),
        P("mod", "tp"),
        P("mod", None),
        P(("mod", "dp"), None),
    )
    return jax.shard_map(
        local,
        mesh=mesh,
        in_specs=placed,
        out_specs=(
            P("mod"),
            P(("mod", "dp"), None, "tp"),
            P(("mod", "dp"), None, "tp"),
            P(("mod", "dp"), "tp"),
            P(("mod", "dp"), None),
            P(("mod", "dp"), None),
        ),
        check_vma=False,
    )
```

```python
import functools

import jax
import jax.numpy as jnp
from jax import lax
from jax.experimental import pallas as pl
from jax.experimental.pallas import tpu as pltpu
from jax.sharding import PartitionSpec as P

HEAD_DIM = 80
EPSILON = 1e-06
LOGIT_SCALE = 1.0 / 0.07
MESH = pl.DeviceIdType.MESH
F32 = jnp.float32
BF16 = jnp.bfloat16

N_MOD, N_DP, N_TP = 4, 16, 2
IMGS = 2
GROUP = N_MOD * IMGS
HEADS = 8
TOK = 257
ROWS = IMGS * TOK
PAD_ROWS = 528
PAD_TOK = PAD_ROWS // IMGS
CHUNK = 176
D = 1280
HALF = D // 2
SLICE = D // N_MOD
OUT_ROWS = SLICE // N_DP
E = 1024
PAIRS = 32
ALL = GROUP * N_DP
SCALE = HEAD_DIM**-0.5
COLUMNS = (512, 512, 640, 640, 640)
ROWS_BY_X = (True, False, False, True, True)
PIECE = SLICE // 4


def dot(a, b):
    return jnp.dot(a, b, preferred_element_type=F32)


def dot_nt(a, b):
    return lax.dot_general(a, b, (((1,), (1,)), ((), ())), preferred_element_type=F32)


def dot_tn(a, b):
    return lax.dot_general(a, b, (((0,), (0,)), ((), ())), preferred_element_type=F32)


def blocks(v):
    return jnp.concatenate(
        [v[:, k : k + 128] for k in range(0, v.shape[1], 128)], axis=0
    )


def unblocks(v):
    n = v.shape[0] * 8
    return jnp.concatenate(
        [v[:, k : k + 8].reshape(n, 128) for k in range(0, v.shape[1], 8)], axis=1
    )


def head_mask():
    lane = lax.broadcasted_iota(jnp.int32, (HEADS, HALF), 1)
    head = lax.broadcasted_iota(jnp.int32, (HEADS, HALF), 0) * HEAD_DIM
    return (lane >= head) & (lane < head + HEAD_DIM)


def expand_heads(v, mask):
    return jnp.concatenate(
        [jnp.where(mask, v[b : b + 1], 0.0) for b in range(GROUP)], axis=0
    ).astype(BF16)


def collapse_heads(v, mask):
    return jnp.concatenate(
        [
            jnp.sum(
                jnp.where(mask, v[b * HEADS : (b + 1) * HEADS], 0.0), axis=0, keepdims=True
            )
            for b in range(GROUP)
        ],
        axis=0,
    )


def row_sum(v):
    return jnp.sum(v, axis=-1, keepdims=True)


def kernel(
    x_hbm, wqkv_hbm, wout_hbm, wproj_hbm, other_hbm,
    loss_ref, gtok_ref, gqkv_ref, gout_ref, gproj_ref, gother_ref,
    other_ref, pairs_ref, x_ref, wq_ref, wp0_ref, wp1_ref, wo_ref, wv_ref, wk_ref,
    xn_ref, mu_ref, inv_ref, grad_ref, dn_ref, dn0_ref, unit_ref, qbd_ref, dbd_ref, hn_ref, dhid_ref,
    s_cls, d_cls, s_oth, d_oth, s_q, d_q, s_kq, d_kq, s_w, d_w, s_ctx, d_ctx, s_att, d_att,
    s_u, d_u, s_cg, d_cg, s_sc, d_sc, s_kv, d_kv,
    f_oth, g_oth, f_emb, g_emb, f_a, g_a, f_b, g_b, f_c, g_c,
    load_sem, y_send, y_recv, b_send, b_recv, a_send, a_recv, core_send, core_recv,
    mod_send, mod_recv, all_send, all_recv, tp_send, tp_recv, dp_send, dp_recv,
):
    m, d, t = lax.axis_index("mod"), lax.axis_index("dp"), lax.axis_index("tp")
    me = t * N_MOD + m
    cx, cz = d // 4, lax.rem(d, 4)
    across = lax.rem(m + 2, N_MOD)
    sibling = m + 1 - 2 * lax.rem(m, 2)

    barrier = pltpu.get_barrier_semaphore()
    for k in range(1, N_MOD):
        pl.semaphore_signal(
            barrier, 1, device_id=(lax.rem(m + k, N_MOD), d, t), device_id_type=MESH
        )
    for k in range(N_MOD):
        pl.semaphore_signal(
            barrier, 1, device_id=(lax.rem(m + k, N_MOD), d, 1 - t), device_id_type=MESH
        )

    def greet(k, carry):
        pl.semaphore_signal(
            barrier, 1, device_id=(m, lax.rem(d + k, N_DP), t), device_id_type=MESH
        )
        return carry

    lax.fori_loop(1, N_DP, greet, 0)

    sources = (
        wproj_hbm.at[:, pl.ds(0, 512)], wproj_hbm.at[:, pl.ds(512, 512)], wout_hbm,
        wqkv_hbm.at[2], wqkv_hbm.at[1],
    )
    gathered = (wp0_ref, wp1_ref, wo_ref, wv_ref, wk_ref)
    load_x = pltpu.make_async_copy(x_hbm, pairs_ref, load_sem.at[6])
    load_x.start()
    load_other = pltpu.make_async_copy(other_hbm, other_ref, load_sem.at[7])
    load_other.start()
    load_q = pltpu.make_async_copy(wqkv_hbm.at[0], wq_ref, load_sem.at[5])
    load_q.start()
    loads = [
        pltpu.make_async_copy(src, dst.at[m], load_sem.at[i])
        for i, (src, dst) in enumerate(zip(sources, gathered))
    ]
    for i in (4, 3, 2, 0, 1):
        loads[i].start()

    leaving = []

    def remote(src, dst, send, recv, peer):
        return pltpu.make_async_remote_copy(
            src, dst, send, recv, device_id=peer, device_id_type=MESH
        )

    def start(copy):
        copy.start()

    def go(copy):
        copy.start()
        leaving.append(copy.wait_send)

    def rows_of(i, step):
        c = cx if ROWS_BY_X[i] else cz
        return pl.ds(pl.multiple_of(lax.rem(c + step, 4) * PIECE, 16), PIECE)

    def cols_of(i, step):
        c = cz if ROWS_BY_X[i] else cx
        return pl.ds(pl.multiple_of(lax.rem(c + step, 4) * 128, 128), 128)

    def row_peer(i, step):
        along_x = (m, lax.rem(cx + step, 4) * 4 + cz, t)
        along_z = (m, cx * 4 + lax.rem(cz + step, 4), t)
        return along_x if ROWS_BY_X[i] else along_z

    def col_peer(i, step):
        along_x = (m, lax.rem(cx + step, 4) * 4 + cz, t)
        along_z = (m, cx * 4 + lax.rem(cz + step, 4), t)
        return along_z if ROWS_BY_X[i] else along_x

    def pieces(i):
        yield 0, cols_of(i, 0)
        if COLUMNS[i] == 640:
            yield 1, pl.ds(512, 128)

    def fetch_core(i):
        go(remote(
            sources[i], gathered[i].at[m], core_send.at[i, 0], core_recv.at[i, 0], (sibling, d, t)
        ))

    def fetch_across(i):
        for n, cols in pieces(i):
            go(remote(
                sources[i].at[rows_of(i, 0), cols], gathered[i].at[m, rows_of(i, 0), cols],
                y_send.at[i, n], y_recv.at[i, n], (across, d, t),
            ))

    def share_cols(i):
        for n, cols in pieces(i):
            part_ref = gathered[i].at[across, rows_of(i, 0), cols]
            remote(
                part_ref, part_ref, y_send.at[i, n], y_recv.at[i, n], (across, d, t)
            ).wait_recv()
        part_ref = gathered[i].at[across, rows_of(i, 0), cols_of(i, 0)]
        for k in (2, 1, 3):
            start(remote(part_ref, part_ref, b_send.at[i], b_recv.at[i], col_peer(i, k)))
        three = gathered[i].at[across, pl.ds(0, PIECE), pl.ds(0, 384)]
        leaving.append(
            remote(three, three, b_send.at[i], b_recv.at[i], col_peer(i, 1)).wait_send
        )

    def share_rows(i):
        three = gathered[i].at[across, pl.ds(0, PIECE), pl.ds(0, 384)]
        remote(three, three, b_send.at[i], b_recv.at[i], col_peer(i, 1)).wait_recv()
        part_ref = gathered[i].at[across, rows_of(i, 0)]
        for k in (2, 1, 3):
            start(remote(part_ref, part_ref, a_send.at[i], a_recv.at[i], row_peer(i, k)))
        three = gathered[i].at[across, pl.ds(0, 3 * PIECE)]
        leaving.append(
            remote(three, three, a_send.at[i], a_recv.at[i], row_peer(i, 1)).wait_send
        )

    def share_core(i):
        three = gathered[i].at[across, pl.ds(0, 3 * PIECE)]
        remote(three, three, a_send.at[i], a_recv.at[i], row_peer(i, 1)).wait_recv()
        block = gathered[i].at[across]
        go(remote(block, block, core_send.at[i, 1], core_recv.at[i, 1], (sibling, d, t)))

    def complete(i):
        for n, owner in ((0, sibling), (1, lax.rem(sibling + 2, N_MOD))):
            block = gathered[i].at[owner]
            remote(
                block, block, core_send.at[i, n], core_recv.at[i, n], (sibling, d, t)
            ).wait_recv()

    def arrivals(dst, count, send, recv, peer):
        ref = dst.at[pl.ds(0, count)]
        return remote(ref, ref, send, recv, peer)

    def mod_all(n, dst):
        return arrivals(dst, N_MOD - 1, mod_send.at[n], mod_recv.at[n], (sibling, d, t))

    def mod_start(n, src, dst):
        for k in (2, 1, 3):
            peer = lax.rem(m + k, N_MOD)
            start(remote(src(peer), dst.at[m], mod_send.at[n], mod_recv.at[n], (peer, d, t)))
        leaving.append(lambda: mod_all(n, dst).wait_send())

    def mod_wait(n, dst):
        mod_all(n, dst).wait_recv()

    def all_all(n, dst):
        return arrivals(dst, 2 * N_MOD - 1, all_send.at[n], all_recv.at[n], (sibling, d, t))

    def all_start(n, src, dst):
        for k in range(2 * N_MOD - 1, 0, -1):
            peer = (lax.rem(m + k, N_MOD), d, t if k < N_MOD else 1 - t)
            start(remote(src, dst.at[me], all_send.at[n], all_recv.at[n], peer))
        leaving.append(lambda: all_all(n, dst).wait_send())

    def all_wait(n, dst):
        all_all(n, dst).wait_recv()

    def dp_all(n, dst):
        return arrivals(
            dst, N_DP - 1, dp_send.at[n], dp_recv.at[n], (m, lax.rem(d + 1, N_DP), t)
        )

    def dp_start(n, src, dst):
        def body(k, carry):
            peer = lax.rem(d + k, N_DP)
            start(remote(src(peer), dst.at[d], dp_send.at[n], dp_recv.at[n], (m, peer, t)))
            return carry

        lax.fori_loop(1, N_DP, body, 0)
        leaving.append(lambda: dp_all(n, dst).wait_send())

    def dp_wait(n, dst):
        dp_all(n, dst).wait_recv()

    def tp_copy(n, src, dst):
        return remote(src, dst, tp_send.at[n], tp_recv.at[n], (m, d, 1 - t))

    def whole(ref):
        return lambda peer: ref

    def part(ref):
        return lambda peer: ref.at[peer]

    row8 = lax.broadcasted_iota(jnp.int32, (GROUP, 1), 0)
    mask = head_mask()

    def place(v):
        return jnp.where(row8 == 2 * m, v[0:1], jnp.where(row8 == 2 * m + 1, v[1:2], 0.0))

    def own_rows(v):
        first = jnp.sum(jnp.where(row8 == 2 * m, v, 0.0), axis=0, keepdims=True)
        second = jnp.sum(jnp.where(row8 == 2 * m + 1, v, 0.0), axis=0, keepdims=True)
        return jnp.where(row8 == 0, first, jnp.where(row8 == 1, second, 0.0))

    def normalise(c):
        at = pl.ds(c * CHUNK, CHUNK)
        x = x_ref[at, :].astype(F32)
        mu = row_sum(x) * (1.0 / D)
        x = x - mu
        inv = lax.rsqrt(row_sum(x * x) * (1.0 / D) + EPSILON)
        xn_ref[at, :] = (x * inv).astype(BF16)
        mu_ref[at, :] = mu
        inv_ref[at, :] = inv

    def window(v, k):
        wide = jnp.concatenate([v, jnp.zeros((v.shape[0], 192), F32)], axis=1)
        return wide[:, k * OUT_ROWS : k * OUT_ROWS + 128]

    def folded(v, k):
        wide = jnp.concatenate([v, jnp.zeros((64, 64), F32)], axis=1)
        at = k * OUT_ROWS
        return jnp.concatenate([wide[0:32, at : at + 64], wide[32:64, at : at + 64]], axis=1)

    def spread(dst, k, v):
        v = expand_heads(v, mask)
        at = pl.ds(pl.multiple_of(k * 32, 32), 32)
        dst[0, at, :] = v[0:32]
        dst[1, at, :] = v[32:64]

    def head_grad(factor, dst):
        factor = factor.reshape(N_DP * 32, 128)
        return dot_tn(factor, dst[0])[0:OUT_ROWS] + dot_tn(factor, dst[1])[64 : 64 + OUT_ROWS]

    def columns(v):
        return [v[:, p * SLICE : (p + 1) * SLICE] for p in range(N_MOD)]

    def full(ref):
        return ref[...].reshape(D, ref.shape[2])

    load_other.wait()
    load_x.wait()
    x8 = pairs_ref[0].astype(F32)
    mu8 = row_sum(x8) * (1.0 / D)
    c8 = x8 - mu8
    n8 = c8 * lax.rsqrt(row_sum(c8 * c8) * (1.0 / D) + EPSILON)
    for p, v in enumerate(columns(jnp.concatenate([place(n8), place(x8)], axis=0))):
        s_cls[p] = v
    d_cls[m] = s_cls[m]
    oth = place(other_ref[...].astype(F32))
    s_oth[...] = oth
    d_oth[m] = oth
    pl.semaphore_wait(barrier, N_MOD - 1 + N_MOD + N_DP - 1)
    mod_start(0, part(s_cls), d_cls)
    for i in (0, 1):
        fetch_across(i)
    for i in (0, 1):
        fetch_core(i)

    def interleave(k, carry):
        rows = pairs_ref[pl.ds(k * 16, 16)].astype(F32).reshape(32, D)
        x_ref[pl.ds(pl.multiple_of(k * 32, 32), 32), :] = rows.astype(BF16)
        return carry

    lax.fori_loop(0, 16, interleave, 0)
    last = jnp.concatenate([pairs_ref[TOK - 1].astype(F32), jnp.zeros((14, D), F32)], axis=0)
    x_ref[512:PAD_ROWS, :] = last.astype(BF16)
    normalise(0)
    load_q.wait()
    mod_wait(0, d_cls)
    cls = d_cls[0] + d_cls[1] + d_cls[2] + d_cls[3]
    n0, x0 = cls[0:8], cls[8:16]

    qp = dot(n0.astype(BF16), wq_ref[...])
    s_q[...] = qp
    d_q[m] = qp
    mod_start(1, whole(s_q), d_q)
    for i in (2, 3, 4):
        fetch_across(i)
    mod_start(2, whole(s_oth), d_oth)
    normalise(1)
    for i in (0, 1):
        share_cols(i)
    loads[4].wait()
    mod_wait(1, d_q)
    q = (d_q[0] + d_q[1] + d_q[2] + d_q[3]).astype(BF16).astype(F32)

    kq = dot_nt(expand_heads(q, mask), wk_ref[m])
    for p in range(N_MOD):
        s_kq[p] = kq[p * 16 : (p + 1) * 16]
    d_kq[m] = s_kq[m]
    mod_start(3, part(s_kq), d_kq)
    for i in (2, 3, 4):
        fetch_core(i)
    normalise(2)
    for i in (2, 3, 4):
        share_cols(i)
    for i in (0, 1):
        share_rows(i)
    mod_wait(3, d_kq)
    kq_b = jnp.concatenate([d_kq[p] for p in range(N_MOD)], axis=1).astype(BF16)

    scores = dot_nt(kq_b, xn_ref[...]) * SCALE
    lane = lax.broadcasted_iota(jnp.int32, (16, PAD_ROWS), 1)
    image = lax.broadcasted_iota(jnp.int32, (16, PAD_ROWS), 0) >= HEADS
    valid = (((lane & 1) == 1) == image) & (lane < ROWS)
    expo = jnp.where(valid, jnp.exp(scores), 0.0)
    soft = expo / row_sum(expo)
    soft_b = soft.astype(BF16)
    w = dot(soft_b, xn_ref[...])
    for p, v in enumerate(columns(w)):
        s_w[p] = v
    d_w[m] = s_w[m]
    mod_start(4, part(s_w), d_w)
    for i in (2, 3, 4):
        share_rows(i)
    mod_wait(2, d_oth)
    oth = blocks(d_oth[0] + d_oth[1] + d_oth[2] + d_oth[3]).astype(BF16)
    f_oth[...] = oth
    g_oth[d] = oth
    dp_start(0, whole(f_oth), g_oth)
    loads[3].wait()
    mod_wait(4, d_w)
    w64 = d_w[...].reshape(64, SLICE)

    cp = collapse_heads(dot(w64.astype(BF16), wv_ref[m]), mask)
    s_ctx[...] = cp
    d_ctx[m] = cp
    mod_start(5, whole(s_ctx), d_ctx)
    loads[2].wait()
    mod_wait(5, d_ctx)
    ctx = d_ctx[0] + d_ctx[1] + d_ctx[2] + d_ctx[3]

    ap = dot_nt(ctx.astype(BF16), wo_ref[m]) + jnp.where(t == 0, x0, 0.0)
    s_att[...] = ap
    d_att[me] = ap
    all_start(0, s_att, d_att)
    common = jnp.concatenate([blocks(q), blocks(ctx), jnp.zeros((8, 128), F32)], axis=0)
    for k in range(N_DP):
        f_a[k] = jnp.concatenate([folded(w64, k), window(n0, k), common], axis=0).astype(BF16)
    g_a[d] = f_a[d]
    loads[0].wait()
    loads[1].wait()
    for i in (0, 1):
        share_core(i)
    all_wait(0, d_att)
    hid = [d_att[p] + d_att[p + N_MOD] for p in range(N_MOD)]
    hmu = sum(row_sum(h) for h in hid) * (1.0 / D)
    hvar = sum(row_sum((h - hmu) * (h - hmu)) for h in hid) * (1.0 / D)
    hinv = lax.rsqrt(hvar + EPSILON)
    for p in range(N_MOD):
        hn_ref[p] = (hid[p] - hmu) * hinv
    hn = jnp.concatenate([hn_ref[p] for p in range(N_MOD)], axis=1)

    hn_b = hn.astype(BF16)
    for i in (0, 1):
        complete(i)
    proj = jnp.concatenate([dot(hn_b, full(wp0_ref)), dot(hn_b, full(wp1_ref))], axis=1)
    pinv = lax.rsqrt(row_sum(proj * proj) + EPSILON)
    embed = proj * pinv
    emb = blocks(embed).astype(BF16)
    f_emb[...] = emb
    g_emb[d] = emb
    dp_start(1, whole(f_emb), g_emb)
    for i in (2, 3, 4):
        share_core(i)
    dp_wait(0, g_oth)
    other_f = unblocks(g_oth[...].astype(F32))
    other_inv = lax.rsqrt(row_sum(other_f * other_f) + EPSILON)
    unit = other_f * other_inv
    unit_ref[...] = unit
    unit_b = unit.astype(BF16)
    dp_start(2, part(f_a), g_a)
    dp_wait(1, g_emb)

    emb_b = unblocks(g_emb[...].astype(F32)).astype(BF16)
    logits = dot_nt(emb_b, unit_b) * LOGIT_SCALE
    left = lax.broadcasted_iota(jnp.int32, (ALL, ALL), 0)
    right = lax.broadcasted_iota(jnp.int32, (ALL, ALL), 1)
    paired = ((left >> 1) & 3) == ((right >> 1) & 3)
    ex = jnp.where(paired, jnp.exp(logits), 0.0)
    row_total = row_sum(ex)
    col_total = jnp.sum(ex, axis=0, keepdims=True)
    grad = (0.5 / PAIRS) * (ex / row_total + ex / col_total)
    grad = grad - jnp.where(left == right, 1.0 / PAIRS, 0.0)
    grad_ref[...] = grad
    grad8 = grad_ref[pl.ds(d * GROUP, GROUP), :].astype(BF16)
    d_embed = LOGIT_SCALE * dot(grad8, unit_b)
    d_proj = (d_embed - embed * row_sum(embed * d_embed)) * pinv
    d_proj_b = d_proj.astype(BF16)
    dh = dot_nt(d_proj_b[:, :512], full(wp0_ref)) + dot_nt(d_proj_b[:, 512:], full(wp1_ref))
    m1 = row_sum(dh) * (1.0 / D)
    m2 = row_sum(dh * hn) * (1.0 / D)
    d_hidden = hinv * (dh - m1 - hn * m2)
    complete(2)
    d_context = dot(d_hidden.astype(BF16), full(wo_ref))

    mine = own_rows(d_context)
    heads = jnp.concatenate(
        [jnp.where(mask, mine[0:1], 0.0), jnp.where(mask, mine[1:2], 0.0)], axis=0
    )
    complete(3)
    vd_b = dot_nt(heads.astype(BF16), full(wv_ref)).astype(BF16)
    d_soft = dot_nt(vd_b, xn_ref[...])
    d_score = soft * (d_soft - row_sum(soft * d_soft))
    d_score_b = d_score.astype(BF16)
    u = dot(d_score_b, xn_ref[...]) * SCALE
    complete(4)
    uk = dot(u.astype(BF16), full(wk_ref))
    dq = place(jnp.concatenate(
        [
            jnp.sum(jnp.where(mask, uk[0:8], 0.0), axis=0, keepdims=True),
            jnp.sum(jnp.where(mask, uk[8:16], 0.0), axis=0, keepdims=True),
        ],
        axis=0,
    ))
    dq = jnp.concatenate([dq[:, :SLICE], dq[:, SLICE:]], axis=0)
    for p, v in enumerate(columns(u)):
        s_u[p] = jnp.concatenate([v, dq], axis=0)
    d_u[m] = s_u[m]
    mod_start(6, part(s_u), d_u)
    s_sc[0:16] = (d_score * SCALE).astype(BF16)
    s_sc[16:32] = soft_b
    s_kv[0:16] = kq_b
    s_kv[16:32] = vd_b
    go(tp_copy(0, s_sc, d_sc))
    go(tp_copy(1, s_kv, d_kv))
    for p, v in enumerate(columns(d_hidden)):
        dhid_ref[p] = v
    hn_m, dhid_m = hn_ref[m], dhid_ref[m]
    common = jnp.concatenate(
        [blocks(d_context), blocks(d_proj), jnp.zeros((8, 128), F32)], axis=0
    )
    for k in range(N_DP):
        f_b[k] = jnp.concatenate([window(hn_m, k), window(dhid_m, k), common], axis=0).astype(
            BF16
        )
    g_b[d] = f_b[d]
    dp_start(3, part(f_b), g_b)
    mod_wait(6, d_u)
    u64 = d_u[:, 0:16].reshape(64, SLICE)
    dq = d_u[0, 16:32] + d_u[1, 16:32] + d_u[2, 16:32] + d_u[3, 16:32]
    dq = jnp.concatenate([dq[0:8], dq[8:16]], axis=1)
    common = jnp.concatenate([blocks(dq), jnp.zeros((8, 128), F32)], axis=0)
    for k in range(N_DP):
        f_c[k] = jnp.concatenate([folded(u64, k), common], axis=0).astype(BF16)
    g_c[d] = f_c[d]
    dp_start(4, part(f_c), g_c)
    cg = dot_nt(dq.astype(BF16), wq_ref[...])
    s_cg[...] = cg
    d_cg[me] = cg
    all_start(1, s_cg, d_cg)

    rows_m = ((lax.broadcasted_iota(jnp.int32, (ALL, 1), 0) >> 1) & 3) == m
    cols_m = ((lax.broadcasted_iota(jnp.int32, (1, ALL), 1) >> 1) & 3) == m
    diag = row_sum(jnp.where(left == right, logits, 0.0))
    loss = jnp.sum(
        jnp.where(rows_m, 0.5 * jnp.log(row_total) - diag, 0.0), axis=0, keepdims=True
    ) + row_sum(jnp.where(cols_m, 0.5 * jnp.log(col_total), 0.0))
    loss_ref[...] = jnp.broadcast_to(loss * (1.0 / PAIRS), (8, 128))
    d_unit = LOGIT_SCALE * dot_tn(grad.astype(BF16), emb_b)
    unit_ref[...] = (d_unit - unit * row_sum(unit * d_unit)) * other_inv
    gother_ref[...] = own_rows(unit_ref[pl.ds(d * GROUP, GROUP), :])[0:IMGS].astype(BF16)

    def spread_q(k, carry):
        spread(qbd_ref, k, unblocks(g_a[pl.ds(k, 1), 40:80].astype(F32)))
        return carry

    dp_wait(2, g_a)
    lax.fori_loop(0, N_DP, spread_q, 0)

    tp_copy(0, s_sc, d_sc).wait_recv()
    tp_copy(1, s_kv, d_kv).wait_recv()
    weights = jnp.concatenate([s_sc[...], d_sc[...]], axis=0).astype(F32).T.astype(BF16)
    factors = jnp.concatenate([s_kv[...], d_kv[...]], axis=0)
    half = pl.ds(pl.multiple_of(t * HALF, 128), HALF)
    for c in range(PAD_ROWS // CHUNK):
        at = pl.ds(c * CHUNK, CHUNK)
        dn = dot(weights[c * CHUNK : (c + 1) * CHUNK], factors)
        mu, inv = mu_ref[at, :], inv_ref[at, :]
        xh = (x_ref[at, :].astype(F32) - mu) * inv
        mean_grad = row_sum(dn) * (1.0 / D)
        mean_cross = row_sum(dn * xh) * (1.0 / D)
        dn_ref[...] = dn
        if c == 0:
            dn0_ref[...] = dn[0:8]
        xh = (x_ref[at, half].astype(F32) - mu) * inv
        grad_x = inv * (dn_ref[:, half] - mean_grad - xh * mean_cross)
        gtok_ref[pl.ds(c * CHUNK // 2, CHUNK // 2)] = grad_x.reshape(CHUNK // 2, IMGS, HALF).astype(
            BF16
        )

    all_wait(1, d_cg)
    extra = own_rows(
        jnp.concatenate([d_cg[p] + d_cg[p + N_MOD] for p in range(N_MOD)], axis=1)
    )
    dn = dn0_ref[...] + extra
    mu, inv = mu_ref[0:8, :], inv_ref[0:8, :]
    xh = (x_ref[0:16, :].astype(F32)[0:8] - mu) * inv
    mean_grad = row_sum(dn) * (1.0 / D)
    mean_cross = row_sum(dn * xh) * (1.0 / D)
    dn0_ref[...] = inv * (dn - mean_grad - xh * mean_cross) + own_rows(d_hidden)
    gtok_ref[0] = dn0_ref[:, half][0:IMGS].astype(BF16)

    def spread_c(k, carry):
        spread(dbd_ref, k, unblocks(g_b[pl.ds(k, 1), 16:56].astype(F32)))
        return carry

    dp_wait(3, g_b)
    lax.fori_loop(0, N_DP, spread_c, 0)
    gqkv_ref[2] = head_grad(g_a[:, 0:32], dbd_ref)
    early = g_a[...].astype(F32)
    late = g_b[...].astype(F32)
    hn_all = unblocks(late[:, 0:8]).astype(BF16)
    dhid_all = unblocks(late[:, 8:16]).astype(BF16)
    gproj_ref[...] = dot_tn(hn_all, unblocks(late[:, 56:120]).astype(BF16))[0:OUT_ROWS]
    gout_ref[...] = dot_tn(dhid_all, unblocks(early[:, 80:120]).astype(BF16))[0:OUT_ROWS]
    n0_all = unblocks(early[:, 32:40]).astype(BF16)
    dp_wait(4, g_c)
    gqkv_ref[1] = head_grad(g_c[:, 0:32], qbd_ref)
    dq_all = unblocks(g_c[...].astype(F32)[:, 32:72]).astype(BF16)
    gqkv_ref[0] = dot_tn(n0_all, dq_all)[0:OUT_ROWS]

    for wait in leaving:
        wait()


def store(*refs):
    sources, targets, sem = refs[:6], refs[6:12], refs[12]
    copies = [
        pltpu.make_async_copy(src, dst, sem.at[k])
        for k, (src, dst) in enumerate(
            [(sources[1].at[pl.ds(0, TOK)], targets[1])] + list(zip(sources[2:], targets[2:]))
        )
    ]
    for copy in copies:
        copy.start()
    targets[0][0] = jnp.max(sources[0][0:1, 0:1])
    for copy in copies:
        copy.wait()


def local(tokens, w_qkv, w_out, w_proj, other_emb):
    vmem = pl.BlockSpec(memory_space=pltpu.VMEM)
    hbm = pl.BlockSpec(memory_space=pltpu.HBM)

    def pair(send, land, dtype=F32):
        return [pltpu.VMEM(send, dtype), pltpu.VMEM(land, dtype)]

    def mod_all(n, k):
        return pair((n, k), (N_MOD, n, k))

    def mod_each(n):
        return pair((N_MOD, n, SLICE), (N_MOD, n, SLICE))

    def dp_all(n):
        return pair((n, 128), (N_DP, n, 128), BF16)

    def dp_each(n):
        return pair((N_DP, n, 128), (N_DP, n, 128), BF16)

    scratch = [pltpu.VMEM((IMGS, E), BF16), pltpu.VMEM((TOK, IMGS, D), BF16), pltpu.VMEM((PAD_ROWS, D), BF16)]
    scratch += [pltpu.VMEM((SLICE, HALF), BF16)]
    scratch += [pltpu.VMEM((N_MOD, SLICE, k), BF16) for k in COLUMNS]
    scratch += [
        pltpu.VMEM((PAD_ROWS, D), BF16),
        pltpu.VMEM((PAD_ROWS, 1), F32),
        pltpu.VMEM((PAD_ROWS, 1), F32),
        pltpu.VMEM((ALL, ALL), F32),
        pltpu.VMEM((CHUNK, D), F32),
        pltpu.VMEM((8, D), F32),
        pltpu.VMEM((ALL, E), F32),
        pltpu.VMEM((2, N_DP * 32, HALF), BF16),
        pltpu.VMEM((2, N_DP * 32, HALF), BF16),
        pltpu.VMEM((N_MOD, GROUP, SLICE), F32),
        pltpu.VMEM((N_MOD, GROUP, SLICE), F32),
    ]
    scratch += mod_each(16) + mod_all(8, E) + mod_all(8, HALF) + mod_each(16) + mod_each(16)
    scratch += mod_all(8, HALF) + pair((8, SLICE), (2 * N_MOD, 8, SLICE))
    scratch += mod_each(32) + pair((8, SLICE), (2 * N_MOD, 8, SLICE))
    scratch += pair((32, PAD_ROWS), (32, PAD_ROWS), BF16) + pair((32, D), (32, D), BF16)
    scratch += dp_all(64) + dp_all(64) + dp_each(128) + dp_each(128) + dp_each(80)
    dma = pltpu.SemaphoreType.DMA
    n = len(COLUMNS)
    scratch += [dma((n + 3,)), dma((n, 2)), dma((n, 2)), dma((n,)), dma((n,))]
    scratch += [dma((n,)), dma((n,)), dma((n, 2)), dma((n, 2))]
    scratch += [dma((7,)), dma((7,)), dma((2,)), dma((2,)), dma((2,)), dma((2,))]
    scratch += [dma((5,)), dma((5,))]

    def shape(*dims, dtype=F32):
        return jax.ShapeDtypeStruct(dims, dtype)

    results = pl.pallas_call(
        kernel,
        out_shape=[
            shape(8, 128),
            shape(PAD_TOK, IMGS, HALF, dtype=BF16),
            shape(3, OUT_ROWS, HALF),
            shape(OUT_ROWS, HALF),
            shape(OUT_ROWS, E),
            shape(IMGS, E, dtype=BF16),
        ],
        in_specs=[hbm] * 5,
        out_specs=[vmem] * 6,
        scratch_shapes=scratch,
        compiler_params=pltpu.CompilerParams(
            collective_id=0, has_side_effects=True, vmem_limit_bytes=48 * 2**20
        ),
    )(
        *(
            pltpu.with_memory_space_constraint(v, pltpu.HBM)
            for v in (
                tokens.transpose(1, 0, 2), w_qkv.transpose(1, 0, 2), w_out, w_proj, other_emb
            )
        )
    )
    loss, grad_tokens, grad_qkv, grad_out, grad_proj, grad_other = pl.pallas_call(
        store,
        out_shape=[
            shape(1),
            shape(TOK, IMGS, HALF, dtype=BF16),
            shape(3, OUT_ROWS, HALF),
            shape(OUT_ROWS, HALF),
            shape(OUT_ROWS, E),
            shape(IMGS, E, dtype=BF16),
        ],
        in_specs=[vmem] * 6,
        out_specs=[pl.BlockSpec(memory_space=pltpu.SMEM)] + [hbm] * 5,
        scratch_shapes=[pltpu.SemaphoreType.DMA((5,))],
        compiler_params=pltpu.CompilerParams(vmem_limit_bytes=16 * 2**20),
    )(*results)
    return (
        loss,
        grad_tokens.transpose(1, 0, 2),
        grad_qkv.transpose(1, 0, 2),
        grad_out,
        grad_proj,
        grad_other,
    )


def solution(mesh):
    placed = (
        P(("mod", "dp"), None, None),
        P("mod", None, "tp"),
        P("mod", "tp"),
        P("mod", None),
        P(("mod", "dp"), None),
    )
    return jax.shard_map(
        local,
        mesh=mesh,
        in_specs=placed,
        out_specs=(
            P("mod"),
            P(("mod", "dp"), None, "tp"),
            P(("mod", "dp"), None, "tp"),
            P(("mod", "dp"), "tp"),
            P(("mod", "dp"), None),
            P(("mod", "dp"), None),
        ),
        check_vma=False,
    )
```

```python
import functools

import jax
import jax.numpy as jnp
from jax import lax
from jax.experimental import pallas as pl
from jax.experimental.pallas import tpu as pltpu
from jax.sharding import PartitionSpec as P

HEAD_DIM = 80
EPSILON = 1e-06
LOGIT_SCALE = 1.0 / 0.07
MESH = pl.DeviceIdType.MESH
F32 = jnp.float32
BF16 = jnp.bfloat16

N_MOD, N_DP, N_TP = 4, 16, 2
IMGS = 2
GROUP = N_MOD * IMGS
HEADS = 8
TOK = 257
ROWS = IMGS * TOK
PAD_ROWS = 528
PAD_TOK = PAD_ROWS // IMGS
CHUNK = 176
D = 1280
HALF = D // 2
SLICE = D // N_MOD
OUT_ROWS = SLICE // N_DP
E = 1024
PAIRS = 32
ALL = GROUP * N_DP
SCALE = HEAD_DIM**-0.5
COLUMNS = (512, 512, 640, 640, 640)
ROWS_BY_X = (True, False, True, False, True)
PIECE = SLICE // 4
FAR_FIRST = sorted(
    [(i, j) for i in range(4) for j in range(4) if i or j],
    key=lambda s: -(min(s[0], 4 - s[0]) + min(s[1], 4 - s[1])),
)


def dot(a, b):
    return jnp.dot(a, b, preferred_element_type=F32)


def dot_nt(a, b):
    return lax.dot_general(a, b, (((1,), (1,)), ((), ())), preferred_element_type=F32)


def dot_tn(a, b):
    return lax.dot_general(a, b, (((0,), (0,)), ((), ())), preferred_element_type=F32)


def blocks(v):
    return jnp.concatenate(
        [v[:, k : k + 128] for k in range(0, v.shape[1], 128)], axis=0
    )


def unblocks(v):
    n = v.shape[0] * 8
    return jnp.concatenate(
        [v[:, k : k + 8].reshape(n, 128) for k in range(0, v.shape[1], 8)], axis=1
    )


def head_mask():
    lane = lax.broadcasted_iota(jnp.int32, (HEADS, HALF), 1)
    head = lax.broadcasted_iota(jnp.int32, (HEADS, HALF), 0) * HEAD_DIM
    return (lane >= head) & (lane < head + HEAD_DIM)


def expand_heads(v, mask):
    return jnp.concatenate(
        [jnp.where(mask, v[b : b + 1], 0.0) for b in range(GROUP)], axis=0
    ).astype(BF16)


def collapse_heads(v, mask):
    return jnp.concatenate(
        [
            jnp.sum(
                jnp.where(mask, v[b * HEADS : (b + 1) * HEADS], 0.0), axis=0, keepdims=True
            )
            for b in range(GROUP)
        ],
        axis=0,
    )


def row_sum(v):
    return jnp.sum(v, axis=-1, keepdims=True)


def kernel(
    x_hbm, wqkv_hbm, wout_hbm, wproj_hbm, other_hbm,
    loss_ref, gtok_ref, gqkv_ref, gout_ref, gproj_ref, gother_ref,
    other_ref, pairs_ref, x_ref, value_ref, wq_ref, wp0_ref, wp1_ref, wo_ref, wv_ref, wk_ref,
    xn_ref, mu_ref, inv_ref, grad_ref, dn_ref, dn0_ref, unit_ref, qbd_ref, dbd_ref, hn_ref, dhid_ref,
    s_cls, d_cls, s_oth, d_oth, s_q, d_q, s_kq, d_kq, s_w, d_w, s_ctx, d_ctx, s_att, d_att,
    s_u, d_u, s_cg, d_cg, s_sc, d_sc, s_kv, d_kv,
    f_oth, g_oth, f_emb, g_emb, f_a, g_a, f_b, g_b, f_c, g_c,
    load_sem, y_send, y_recv, b_send, b_recv, a_send, a_recv, core_send, core_recv,
    mod_send, mod_recv, all_send, all_recv, tp_send, tp_recv, dp_send, dp_recv,
):
    m, d, t = lax.axis_index("mod"), lax.axis_index("dp"), lax.axis_index("tp")
    me = t * N_MOD + m
    cx, cz = d // 4, lax.rem(d, 4)
    across = lax.rem(m + 2, N_MOD)
    sibling = m + 1 - 2 * lax.rem(m, 2)

    barrier = pltpu.get_barrier_semaphore()
    for k in range(1, N_MOD):
        pl.semaphore_signal(
            barrier, 1, device_id=(lax.rem(m + k, N_MOD), d, t), device_id_type=MESH
        )
    for k in range(N_MOD):
        pl.semaphore_signal(
            barrier, 1, device_id=(lax.rem(m + k, N_MOD), d, 1 - t), device_id_type=MESH
        )

    def greet(k, carry):
        pl.semaphore_signal(
            barrier, 1, device_id=(m, lax.rem(d + k, N_DP), t), device_id_type=MESH
        )
        return carry

    lax.fori_loop(1, N_DP, greet, 0)

    sources = (
        wproj_hbm.at[:, pl.ds(0, 512)], wproj_hbm.at[:, pl.ds(512, 512)], wout_hbm,
        wqkv_hbm.at[2], wqkv_hbm.at[1],
    )
    gathered = (wp0_ref, wp1_ref, wo_ref, wv_ref, wk_ref)
    load_x = pltpu.make_async_copy(x_hbm, pairs_ref, load_sem.at[6])
    load_x.start()
    load_other = pltpu.make_async_copy(other_hbm, other_ref, load_sem.at[7])
    load_other.start()
    load_q = pltpu.make_async_copy(wqkv_hbm.at[0], wq_ref, load_sem.at[5])
    load_q.start()
    loads = [
        pltpu.make_async_copy(src, dst.at[m], load_sem.at[i])
        for i, (src, dst) in enumerate(zip(sources, gathered))
    ]
    for i in (4, 3, 2, 0, 1):
        loads[i].start()

    leaving = []

    def remote(src, dst, send, recv, peer):
        return pltpu.make_async_remote_copy(
            src, dst, send, recv, device_id=peer, device_id_type=MESH
        )

    def start(copy):
        copy.start()

    def go(copy):
        copy.start()
        leaving.append(copy.wait_send)

    def rows_of(i, step):
        c = cx if ROWS_BY_X[i] else cz
        return pl.ds(pl.multiple_of(lax.rem(c + step, 4) * PIECE, 16), PIECE)

    def cols_of(i, step):
        c = cz if ROWS_BY_X[i] else cx
        return pl.ds(pl.multiple_of(lax.rem(c + step, 4) * 128, 128), 128)

    def row_peer(i, step):
        along_x = (m, lax.rem(cx + step, 4) * 4 + cz, t)
        along_z = (m, cx * 4 + lax.rem(cz + step, 4), t)
        return along_x if ROWS_BY_X[i] else along_z

    def col_peer(i, step):
        along_x = (m, lax.rem(cx + step, 4) * 4 + cz, t)
        along_z = (m, cx * 4 + lax.rem(cz + step, 4), t)
        return along_z if ROWS_BY_X[i] else along_x

    def pieces(i):
        yield 0, cols_of(i, 0)
        if COLUMNS[i] == 640:
            yield 1, pl.ds(512, 128)

    def fetch_core(i):
        go(remote(
            sources[i], gathered[i].at[m], core_send.at[i, 0], core_recv.at[i, 0], (sibling, d, t)
        ))

    def fetch_across(i):
        for n, cols in pieces(i):
            go(remote(
                sources[i].at[rows_of(i, 0), cols], gathered[i].at[m, rows_of(i, 0), cols],
                y_send.at[i, n], y_recv.at[i, n], (across, d, t),
            ))

    def share_cols(i):
        for n, cols in pieces(i):
            part_ref = gathered[i].at[across, rows_of(i, 0), cols]
            remote(
                part_ref, part_ref, y_send.at[i, n], y_recv.at[i, n], (across, d, t)
            ).wait_recv()
        part_ref = gathered[i].at[across, rows_of(i, 0), cols_of(i, 0)]
        for k in (2, 1, 3):
            start(remote(part_ref, part_ref, b_send.at[i], b_recv.at[i], col_peer(i, k)))
        three = gathered[i].at[across, pl.ds(0, PIECE), pl.ds(0, 384)]
        leaving.append(
            remote(three, three, b_send.at[i], b_recv.at[i], col_peer(i, 1)).wait_send
        )

    def share_rows(i):
        three = gathered[i].at[across, pl.ds(0, PIECE), pl.ds(0, 384)]
        remote(three, three, b_send.at[i], b_recv.at[i], col_peer(i, 1)).wait_recv()
        part_ref = gathered[i].at[across, rows_of(i, 0)]
        for k in (2, 1, 3):
            start(remote(part_ref, part_ref, a_send.at[i], a_recv.at[i], row_peer(i, k)))
        three = gathered[i].at[across, pl.ds(0, 3 * PIECE)]
        leaving.append(
            remote(three, three, a_send.at[i], a_recv.at[i], row_peer(i, 1)).wait_send
        )

    def share_core(i):
        three = gathered[i].at[across, pl.ds(0, 3 * PIECE)]
        remote(three, three, a_send.at[i], a_recv.at[i], row_peer(i, 1)).wait_recv()
        block = gathered[i].at[across]
        go(remote(block, block, core_send.at[i, 1], core_recv.at[i, 1], (sibling, d, t)))

    def complete(i):
        for n, owner in ((0, sibling), (1, lax.rem(sibling + 2, N_MOD))):
            block = gathered[i].at[owner]
            remote(
                block, block, core_send.at[i, n], core_recv.at[i, n], (sibling, d, t)
            ).wait_recv()

    def arrivals(dst, count, send, recv, peer):
        ref = dst.at[pl.ds(0, count)]
        return remote(ref, ref, send, recv, peer)

    def mod_all(n, dst):
        return arrivals(dst, N_MOD - 1, mod_send.at[n], mod_recv.at[n], (sibling, d, t))

    def mod_start(n, src, dst):
        for k in (2, 1, 3):
            peer = lax.rem(m + k, N_MOD)
            start(remote(src(peer), dst.at[m], mod_send.at[n], mod_recv.at[n], (peer, d, t)))
        leaving.append(lambda: mod_all(n, dst).wait_send())

    def mod_wait(n, dst):
        mod_all(n, dst).wait_recv()

    def all_all(n, dst):
        return arrivals(dst, 2 * N_MOD - 1, all_send.at[n], all_recv.at[n], (sibling, d, t))

    def all_start(n, src, dst):
        for k in range(2 * N_MOD - 1, 0, -1):
            peer = (lax.rem(m + k, N_MOD), d, t if k < N_MOD else 1 - t)
            start(remote(src, dst.at[me], all_send.at[n], all_recv.at[n], peer))
        leaving.append(lambda: all_all(n, dst).wait_send())

    def all_wait(n, dst):
        all_all(n, dst).wait_recv()

    def dp_all(n, dst):
        return arrivals(
            dst, N_DP - 1, dp_send.at[n], dp_recv.at[n], (m, lax.rem(d + 1, N_DP), t)
        )

    def dp_start(n, src, dst):
        def body(k, carry):
            peer = lax.rem(d + k, N_DP)
            start(remote(src(peer), dst.at[d], dp_send.at[n], dp_recv.at[n], (m, peer, t)))
            return carry

        lax.fori_loop(1, N_DP, body, 0)
        leaving.append(lambda: dp_all(n, dst).wait_send())

    def dp_start_far(n, src, dst):
        for i, j in FAR_FIRST:
            peer = lax.rem(cx + i, 4) * 4 + lax.rem(cz + j, 4)
            start(remote(src(peer), dst.at[d], dp_send.at[n], dp_recv.at[n], (m, peer, t)))
        leaving.append(lambda: dp_all(n, dst).wait_send())

    def dp_wait(n, dst):
        dp_all(n, dst).wait_recv()

    def tp_copy(n, src, dst):
        return remote(src, dst, tp_send.at[n], tp_recv.at[n], (m, d, 1 - t))

    def whole(ref):
        return lambda peer: ref

    def part(ref):
        return lambda peer: ref.at[peer]

    row8 = lax.broadcasted_iota(jnp.int32, (GROUP, 1), 0)
    mask = head_mask()

    def place(v):
        return jnp.where(row8 == 2 * m, v[0:1], jnp.where(row8 == 2 * m + 1, v[1:2], 0.0))

    def own_rows(v):
        first = jnp.sum(jnp.where(row8 == 2 * m, v, 0.0), axis=0, keepdims=True)
        second = jnp.sum(jnp.where(row8 == 2 * m + 1, v, 0.0), axis=0, keepdims=True)
        return jnp.where(row8 == 0, first, jnp.where(row8 == 1, second, 0.0))

    def normalise(c):
        at = pl.ds(c * CHUNK, CHUNK)
        x = x_ref[at, :].astype(F32)
        mu = row_sum(x) * (1.0 / D)
        x = x - mu
        inv = lax.rsqrt(row_sum(x * x) * (1.0 / D) + EPSILON)
        xn_ref[at, :] = (x * inv).astype(BF16)
        mu_ref[at, :] = mu
        inv_ref[at, :] = inv

    def window(v, k):
        wide = jnp.concatenate([v, jnp.zeros((v.shape[0], 192), F32)], axis=1)
        return wide[:, k * OUT_ROWS : k * OUT_ROWS + 128]

    def folded(v, k):
        wide = jnp.concatenate([v, jnp.zeros((64, 64), F32)], axis=1)
        at = k * OUT_ROWS
        return jnp.concatenate([wide[0:32, at : at + 64], wide[32:64, at : at + 64]], axis=1)

    def spread(dst, k, v):
        v = expand_heads(v, mask)
        at = pl.ds(pl.multiple_of(k * 32, 32), 32)
        dst[0, at, :] = v[0:32]
        dst[1, at, :] = v[32:64]

    def head_grad(factor, dst):
        factor = factor.reshape(N_DP * 32, 128)
        return dot_tn(factor, dst[0])[0:OUT_ROWS] + dot_tn(factor, dst[1])[64 : 64 + OUT_ROWS]

    def columns(v):
        return [v[:, p * SLICE : (p + 1) * SLICE] for p in range(N_MOD)]

    def full(ref):
        return ref[...].reshape(D, ref.shape[2])

    load_other.wait()
    load_x.wait()
    x8 = pairs_ref[0].astype(F32)
    mu8 = row_sum(x8) * (1.0 / D)
    c8 = x8 - mu8
    n8 = c8 * lax.rsqrt(row_sum(c8 * c8) * (1.0 / D) + EPSILON)
    for p, v in enumerate(columns(jnp.concatenate([place(n8), place(x8)], axis=0))):
        s_cls[p] = v
    d_cls[m] = s_cls[m]
    oth = blocks(place(other_ref[...].astype(F32))).astype(BF16)
    s_oth[...] = oth
    d_oth[m] = oth
    pl.semaphore_wait(barrier, N_MOD - 1 + N_MOD + N_DP - 1)
    mod_start(0, part(s_cls), d_cls)
    for i in range(5):
        fetch_across(i)
    for i in (0, 1):
        fetch_core(i)

    def interleave(k, carry):
        rows = pairs_ref[pl.ds(k * 16, 16)].astype(F32).reshape(32, D)
        x_ref[pl.ds(pl.multiple_of(k * 32, 32), 32), :] = rows.astype(BF16)
        return carry

    lax.fori_loop(0, 16, interleave, 0)
    last = jnp.concatenate([pairs_ref[TOK - 1].astype(F32), jnp.zeros((14, D), F32)], axis=0)
    x_ref[512:PAD_ROWS, :] = last.astype(BF16)
    normalise(0)
    load_q.wait()
    mod_wait(0, d_cls)
    cls = d_cls[0] + d_cls[1] + d_cls[2] + d_cls[3]
    n0, x0 = cls[0:8], cls[8:16]

    qp = dot(n0.astype(BF16), wq_ref[...])
    s_q[...] = qp
    d_q[m] = qp
    mod_start(1, whole(s_q), d_q)
    for i in (0, 1):
        share_cols(i)
    normalise(1)
    for i in (2, 3, 4):
        share_cols(i)
    loads[4].wait()
    mod_wait(1, d_q)
    q = (d_q[0] + d_q[1] + d_q[2] + d_q[3]).astype(BF16).astype(F32)

    kq = dot_nt(expand_heads(q, mask), wk_ref[m])
    for p in range(N_MOD):
        s_kq[p] = kq[p * 16 : (p + 1) * 16]
    d_kq[m] = s_kq[m]
    mod_start(3, part(s_kq), d_kq)
    mod_start(2, whole(s_oth), d_oth)
    for i in (2, 3, 4):
        fetch_core(i)
    normalise(2)
    for i in range(5):
        share_rows(i)
    mod_wait(3, d_kq)
    kq_b = jnp.concatenate([d_kq[p] for p in range(N_MOD)], axis=1).astype(BF16)

    scores = dot_nt(kq_b, xn_ref[...]) * SCALE
    lane = lax.broadcasted_iota(jnp.int32, (16, PAD_ROWS), 1)
    image = lax.broadcasted_iota(jnp.int32, (16, PAD_ROWS), 0) >= HEADS
    valid = (((lane & 1) == 1) == image) & (lane < ROWS)
    expo = jnp.where(valid, jnp.exp(scores), 0.0)
    soft = expo / row_sum(expo)
    soft_b = soft.astype(BF16)
    w = dot(soft_b, xn_ref[...])
    for p, v in enumerate(columns(w)):
        s_w[p] = v
    d_w[m] = s_w[m]
    mod_start(4, part(s_w), d_w)
    mod_wait(2, d_oth)
    oth = d_oth[0].astype(F32) + d_oth[1].astype(F32)
    oth = (oth + d_oth[2].astype(F32) + d_oth[3].astype(F32)).astype(BF16)
    f_oth[...] = oth
    g_oth[d] = oth
    loads[3].wait()
    mod_wait(4, d_w)
    w64 = d_w[...].reshape(64, SLICE)

    cp = collapse_heads(dot(w64.astype(BF16), wv_ref[m]), mask)
    s_ctx[...] = cp
    d_ctx[m] = cp
    mod_start(5, whole(s_ctx), d_ctx)
    dp_start(0, whole(f_oth), g_oth)
    loads[2].wait()
    mod_wait(5, d_ctx)
    ctx = d_ctx[0] + d_ctx[1] + d_ctx[2] + d_ctx[3]

    ap = dot_nt(ctx.astype(BF16), wo_ref[m]) + jnp.where(t == 0, x0, 0.0)
    s_att[...] = ap
    d_att[me] = ap
    all_start(0, s_att, d_att)
    loads[0].wait()
    loads[1].wait()
    for i in (0, 1):
        share_core(i)
    all_wait(0, d_att)
    hid = [d_att[p] + d_att[p + N_MOD] for p in range(N_MOD)]
    hmu = sum(row_sum(h) for h in hid) * (1.0 / D)
    hvar = sum(row_sum((h - hmu) * (h - hmu)) for h in hid) * (1.0 / D)
    hinv = lax.rsqrt(hvar + EPSILON)
    for p in range(N_MOD):
        hn_ref[p] = (hid[p] - hmu) * hinv
    hn = jnp.concatenate([hn_ref[p] for p in range(N_MOD)], axis=1)

    hn_b = hn.astype(BF16)
    for i in (0, 1):
        complete(i)
    proj = jnp.concatenate([dot(hn_b, full(wp0_ref)), dot(hn_b, full(wp1_ref))], axis=1)
    pinv = lax.rsqrt(row_sum(proj * proj) + EPSILON)
    embed = proj * pinv
    emb = blocks(embed).astype(BF16)
    f_emb[...] = emb
    g_emb[d] = emb
    dp_start_far(1, whole(f_emb), g_emb)
    for i in (3, 2, 4):
        share_core(i)
    hn_m = hn_ref[m]
    common = jnp.concatenate([blocks(q), blocks(ctx)], axis=0)
    for k in range(N_DP):
        f_a[k] = jnp.concatenate(
            [folded(w64, k), window(n0, k), window(hn_m, k), common], axis=0
        ).astype(BF16)
    g_a[d] = f_a[d]
    dp_wait(0, g_oth)
    other_f = unblocks(g_oth[...].astype(F32))
    other_inv = lax.rsqrt(row_sum(other_f * other_f) + EPSILON)
    unit = other_f * other_inv
    unit_ref[...] = unit
    unit_b = unit.astype(BF16)
    dp_start(2, part(f_a), g_a)
    complete(3)
    for c in range(PAD_ROWS // CHUNK):
        at = pl.ds(c * CHUNK, CHUNK)
        value_ref[at, :] = dot(xn_ref[at, :], full(wv_ref)).astype(BF16)
    dp_wait(1, g_emb)

    emb_b = unblocks(g_emb[...].astype(F32)).astype(BF16)
    logits = dot_nt(emb_b, unit_b) * LOGIT_SCALE
    left = lax.broadcasted_iota(jnp.int32, (ALL, ALL), 0)
    right = lax.broadcasted_iota(jnp.int32, (ALL, ALL), 1)
    paired = ((left >> 1) & 3) == ((right >> 1) & 3)
    ex = jnp.where(paired, jnp.exp(logits), 0.0)
    row_total = row_sum(ex)
    col_total = jnp.sum(ex, axis=0, keepdims=True)
    grad = (0.5 / PAIRS) * (ex / row_total + ex / col_total)
    grad = grad - jnp.where(left == right, 1.0 / PAIRS, 0.0)
    grad_ref[...] = grad
    grad8 = grad_ref[pl.ds(d * GROUP, GROUP), :].astype(BF16)
    d_embed = LOGIT_SCALE * dot(grad8, unit_b)
    d_proj = (d_embed - embed * row_sum(embed * d_embed)) * pinv
    d_proj_b = d_proj.astype(BF16)
    dh = dot_nt(d_proj_b[:, :512], full(wp0_ref)) + dot_nt(d_proj_b[:, 512:], full(wp1_ref))
    m1 = row_sum(dh) * (1.0 / D)
    m2 = row_sum(dh * hn) * (1.0 / D)
    d_hidden = hinv * (dh - m1 - hn * m2)
    complete(2)
    d_context = dot(d_hidden.astype(BF16), full(wo_ref))

    mine = own_rows(d_context)
    heads = jnp.concatenate(
        [jnp.where(mask, mine[0:1], 0.0), jnp.where(mask, mine[1:2], 0.0)], axis=0
    ).astype(BF16)
    d_soft = dot_nt(heads, value_ref[...])
    d_score = soft * (d_soft - row_sum(soft * d_soft))
    d_score_b = d_score.astype(BF16)
    u = dot(d_score_b, xn_ref[...]) * SCALE
    complete(4)
    uk = dot(u.astype(BF16), full(wk_ref))
    dq = place(jnp.concatenate(
        [
            jnp.sum(jnp.where(mask, uk[0:8], 0.0), axis=0, keepdims=True),
            jnp.sum(jnp.where(mask, uk[8:16], 0.0), axis=0, keepdims=True),
        ],
        axis=0,
    ))
    dq = jnp.concatenate([dq[:, :SLICE], dq[:, SLICE:]], axis=0)
    for p, v in enumerate(columns(u)):
        s_u[p] = jnp.concatenate([v, dq], axis=0)
    d_u[m] = s_u[m]
    mod_start(6, part(s_u), d_u)
    vd_b = dot_nt(heads, full(wv_ref)).astype(BF16)
    s_sc[0:16] = (d_score * SCALE).astype(BF16)
    s_sc[16:32] = soft_b
    s_kv[0:16] = kq_b
    s_kv[16:32] = vd_b
    go(tp_copy(0, s_sc, d_sc))
    go(tp_copy(1, s_kv, d_kv))
    for p, v in enumerate(columns(d_hidden)):
        dhid_ref[p] = v
    dhid_m = dhid_ref[m]
    high = pinv.astype(BF16).astype(F32)
    lane = lax.broadcasted_iota(jnp.int32, (GROUP, 128), 1)
    common = jnp.concatenate(
        [jnp.where(lane < 64, high, pinv - high), blocks(d_context), jnp.zeros((8, 128), F32)],
        axis=0,
    )
    for k in range(N_DP):
        f_b[k] = jnp.concatenate([window(dhid_m, k), common], axis=0).astype(BF16)
    g_b[d] = f_b[d]
    dp_start(3, part(f_b), g_b)
    mod_wait(6, d_u)
    u64 = d_u[:, 0:16].reshape(64, SLICE)
    dq = d_u[0, 16:32] + d_u[1, 16:32] + d_u[2, 16:32] + d_u[3, 16:32]
    dq = jnp.concatenate([dq[0:8], dq[8:16]], axis=1)
    common = jnp.concatenate([blocks(dq), jnp.zeros((8, 128), F32)], axis=0)
    for k in range(N_DP):
        f_c[k] = jnp.concatenate([folded(u64, k), common], axis=0).astype(BF16)
    g_c[d] = f_c[d]
    dp_start_far(4, part(f_c), g_c)
    cg = dot_nt(dq.astype(BF16), wq_ref[...])
    s_cg[...] = cg
    d_cg[me] = cg
    all_start(1, s_cg, d_cg)

    rows_m = ((lax.broadcasted_iota(jnp.int32, (ALL, 1), 0) >> 1) & 3) == m
    cols_m = ((lax.broadcasted_iota(jnp.int32, (1, ALL), 1) >> 1) & 3) == m
    diag = row_sum(jnp.where(left == right, logits, 0.0))
    loss = jnp.sum(
        jnp.where(rows_m, 0.5 * jnp.log(row_total) - diag, 0.0), axis=0, keepdims=True
    ) + row_sum(jnp.where(cols_m, 0.5 * jnp.log(col_total), 0.0))
    loss_ref[...] = jnp.broadcast_to(loss * (1.0 / PAIRS), (8, 128))
    d_unit = LOGIT_SCALE * dot_tn(grad.astype(BF16), emb_b)
    unit_ref[...] = (d_unit - unit * row_sum(unit * d_unit)) * other_inv
    gother_ref[...] = own_rows(unit_ref[pl.ds(d * GROUP, GROUP), :])[0:IMGS].astype(BF16)

    def spread_q(k, carry):
        spread(qbd_ref, k, unblocks(g_a[pl.ds(k, 1), 48:88].astype(F32)))
        return carry

    dp_wait(2, g_a)
    lax.fori_loop(0, N_DP, spread_q, 0)

    tp_copy(0, s_sc, d_sc).wait_recv()
    tp_copy(1, s_kv, d_kv).wait_recv()
    weights = jnp.concatenate([s_sc[...], d_sc[...]], axis=0).astype(F32).T.astype(BF16)
    factors = jnp.concatenate([s_kv[...], d_kv[...]], axis=0)
    half = pl.ds(pl.multiple_of(t * HALF, 128), HALF)
    for c in range(PAD_ROWS // CHUNK):
        at = pl.ds(c * CHUNK, CHUNK)
        dn = dot(weights[c * CHUNK : (c + 1) * CHUNK], factors)
        mu, inv = mu_ref[at, :], inv_ref[at, :]
        xh = (x_ref[at, :].astype(F32) - mu) * inv
        mean_grad = row_sum(dn) * (1.0 / D)
        mean_cross = row_sum(dn * xh) * (1.0 / D)
        dn_ref[...] = dn
        if c == 0:
            dn0_ref[...] = dn[0:8]
        xh = (x_ref[at, half].astype(F32) - mu) * inv
        grad_x = inv * (dn_ref[:, half] - mean_grad - xh * mean_cross)
        gtok_ref[pl.ds(c * CHUNK // 2, CHUNK // 2)] = grad_x.reshape(CHUNK // 2, IMGS, HALF).astype(
            BF16
        )

    all_wait(1, d_cg)
    extra = own_rows(
        jnp.concatenate([d_cg[p] + d_cg[p + N_MOD] for p in range(N_MOD)], axis=1)
    )
    dn = dn0_ref[...] + extra
    mu, inv = mu_ref[0:8, :], inv_ref[0:8, :]
    xh = (x_ref[0:16, :].astype(F32)[0:8] - mu) * inv
    mean_grad = row_sum(dn) * (1.0 / D)
    mean_cross = row_sum(dn * xh) * (1.0 / D)
    dn0_ref[...] = inv * (dn - mean_grad - xh * mean_cross) + own_rows(d_hidden)
    gtok_ref[0] = dn0_ref[:, half][0:IMGS].astype(BF16)

    def spread_c(k, carry):
        spread(dbd_ref, k, unblocks(g_b[pl.ds(k, 1), 16:56].astype(F32)))
        return carry

    dp_wait(3, g_b)
    lax.fori_loop(0, N_DP, spread_c, 0)
    gqkv_ref[2] = head_grad(g_a[:, 0:32], dbd_ref)
    early = g_a[...].astype(F32)
    late = g_b[...].astype(F32)
    dhid_all = unblocks(late[:, 0:8]).astype(BF16)
    gout_ref[...] = dot_tn(dhid_all, unblocks(early[:, 88:128]).astype(BF16))[0:OUT_ROWS]
    pinv_all = unblocks(late[:, 8:16])
    pinv_all = pinv_all[:, 0:1] + pinv_all[:, 64:65]
    emb = emb_b.astype(F32)
    d_embed = LOGIT_SCALE * dot(grad.astype(BF16), unit_b)
    d_proj = (d_embed - emb * row_sum(emb * d_embed)) * pinv_all
    hn_all = unblocks(early[:, 40:48]).astype(BF16)
    gproj_ref[...] = dot_tn(hn_all, d_proj.astype(BF16))[0:OUT_ROWS]
    n0_all = unblocks(early[:, 32:40]).astype(BF16)
    dp_wait(4, g_c)
    gqkv_ref[1] = head_grad(g_c[:, 0:32], qbd_ref)
    dq_all = unblocks(g_c[...].astype(F32)[:, 32:72]).astype(BF16)
    gqkv_ref[0] = dot_tn(n0_all, dq_all)[0:OUT_ROWS]

    for wait in leaving:
        wait()


def store(*refs):
    sources, targets, sem = refs[:6], refs[6:12], refs[12]
    copies = [
        pltpu.make_async_copy(src, dst, sem.at[k])
        for k, (src, dst) in enumerate(
            [(sources[1].at[pl.ds(0, TOK)], targets[1])] + list(zip(sources[2:], targets[2:]))
        )
    ]
    for copy in copies:
        copy.start()
    targets[0][0] = jnp.max(sources[0][0:1, 0:1])
    for copy in copies:
        copy.wait()


def local(tokens, w_qkv, w_out, w_proj, other_emb):
    vmem = pl.BlockSpec(memory_space=pltpu.VMEM)
    hbm = pl.BlockSpec(memory_space=pltpu.HBM)

    def pair(send, land, dtype=F32):
        return [pltpu.VMEM(send, dtype), pltpu.VMEM(land, dtype)]

    def mod_all(n, k):
        return pair((n, k), (N_MOD, n, k))

    def mod_each(n):
        return pair((N_MOD, n, SLICE), (N_MOD, n, SLICE))

    def dp_all(n):
        return pair((n, 128), (N_DP, n, 128), BF16)

    def dp_each(n):
        return pair((N_DP, n, 128), (N_DP, n, 128), BF16)

    scratch = [pltpu.VMEM((IMGS, E), BF16), pltpu.VMEM((TOK, IMGS, D), BF16), pltpu.VMEM((PAD_ROWS, D), BF16)]
    scratch += [pltpu.VMEM((PAD_ROWS, HALF), BF16)]
    scratch += [pltpu.VMEM((SLICE, HALF), BF16)]
    scratch += [pltpu.VMEM((N_MOD, SLICE, k), BF16) for k in COLUMNS]
    scratch += [
        pltpu.VMEM((PAD_ROWS, D), BF16),
        pltpu.VMEM((PAD_ROWS, 1), F32),
        pltpu.VMEM((PAD_ROWS, 1), F32),
        pltpu.VMEM((ALL, ALL), F32),
        pltpu.VMEM((CHUNK, D), F32),
        pltpu.VMEM((8, D), F32),
        pltpu.VMEM((ALL, E), F32),
        pltpu.VMEM((2, N_DP * 32, HALF), BF16),
        pltpu.VMEM((2, N_DP * 32, HALF), BF16),
        pltpu.VMEM((N_MOD, GROUP, SLICE), F32),
        pltpu.VMEM((N_MOD, GROUP, SLICE), F32),
    ]
    scratch += mod_each(16) + pair((64, 128), (N_MOD, 64, 128), BF16) + mod_all(8, HALF) + mod_each(16) + mod_each(16)
    scratch += mod_all(8, HALF) + pair((8, SLICE), (2 * N_MOD, 8, SLICE))
    scratch += mod_each(32) + pair((8, SLICE), (2 * N_MOD, 8, SLICE))
    scratch += pair((32, PAD_ROWS), (32, PAD_ROWS), BF16) + pair((32, D), (32, D), BF16)
    scratch += dp_all(64) + dp_all(64) + dp_each(128) + dp_each(64) + dp_each(80)
    dma = pltpu.SemaphoreType.DMA
    n = len(COLUMNS)
    scratch += [dma((n + 3,)), dma((n, 2)), dma((n, 2)), dma((n,)), dma((n,))]
    scratch += [dma((n,)), dma((n,)), dma((n, 2)), dma((n, 2))]
    scratch += [dma((7,)), dma((7,)), dma((2,)), dma((2,)), dma((2,)), dma((2,))]
    scratch += [dma((5,)), dma((5,))]

    def shape(*dims, dtype=F32):
        return jax.ShapeDtypeStruct(dims, dtype)

    results = pl.pallas_call(
        kernel,
        out_shape=[
            shape(8, 128),
            shape(PAD_TOK, IMGS, HALF, dtype=BF16),
            shape(3, OUT_ROWS, HALF),
            shape(OUT_ROWS, HALF),
            shape(OUT_ROWS, E),
            shape(IMGS, E, dtype=BF16),
        ],
        in_specs=[hbm] * 5,
        out_specs=[vmem] * 6,
        scratch_shapes=scratch,
        compiler_params=pltpu.CompilerParams(
            collective_id=0, has_side_effects=True, vmem_limit_bytes=48 * 2**20
        ),
    )(
        *(
            pltpu.with_memory_space_constraint(v, pltpu.HBM)
            for v in (
                tokens.transpose(1, 0, 2), w_qkv.transpose(1, 0, 2), w_out, w_proj, other_emb
            )
        )
    )
    loss, grad_tokens, grad_qkv, grad_out, grad_proj, grad_other = pl.pallas_call(
        store,
        out_shape=[
            shape(1),
            shape(TOK, IMGS, HALF, dtype=BF16),
            shape(3, OUT_ROWS, HALF),
            shape(OUT_ROWS, HALF),
            shape(OUT_ROWS, E),
            shape(IMGS, E, dtype=BF16),
        ],
        in_specs=[vmem] * 6,
        out_specs=[pl.BlockSpec(memory_space=pltpu.SMEM)] + [hbm] * 5,
        scratch_shapes=[pltpu.SemaphoreType.DMA((5,))],
        compiler_params=pltpu.CompilerParams(vmem_limit_bytes=16 * 2**20),
    )(*results)
    return (
        loss,
        grad_tokens.transpose(1, 0, 2),
        grad_qkv.transpose(1, 0, 2),
        grad_out,
        grad_proj,
        grad_other,
    )


def solution(mesh):
    placed = (
        P(("mod", "dp"), None, None),
        P("mod", None, "tp"),
        P("mod", "tp"),
        P("mod", None),
        P(("mod", "dp"), None),
    )
    return jax.shard_map(
        local,
        mesh=mesh,
        in_specs=placed,
        out_specs=(
            P("mod"),
            P(("mod", "dp"), None, "tp"),
            P(("mod", "dp"), None, "tp"),
            P(("mod", "dp"), "tp"),
            P(("mod", "dp"), None),
            P(("mod", "dp"), None),
        ),
        check_vma=False,
    )
```

```python
import functools

import jax
import jax.numpy as jnp
from jax import lax
from jax.experimental import pallas as pl
from jax.experimental.pallas import tpu as pltpu
from jax.sharding import PartitionSpec as P

HEAD_DIM = 80
EPSILON = 1e-06
LOGIT_SCALE = 1.0 / 0.07
MESH = pl.DeviceIdType.MESH
F32 = jnp.float32
BF16 = jnp.bfloat16

N_MOD, N_DP, N_TP = 4, 16, 2
IMGS = 2
GROUP = N_MOD * IMGS
HEADS = 8
TOK = 257
ROWS = IMGS * TOK
PAD_ROWS = 528
PAD_TOK = PAD_ROWS // IMGS
CHUNK = 176
D = 1280
HALF = D // 2
SLICE = D // N_MOD
OUT_ROWS = SLICE // N_DP
E = 1024
PAIRS = 32
ALL = GROUP * N_DP
SCALE = HEAD_DIM**-0.5
COLUMNS = (512, 512, 640, 640, 640)
ROWS_BY_X = (True, False, True, False, True)
PIECE = SLICE // 4
FAR_FIRST = sorted(
    [(i, j) for i in range(4) for j in range(4) if i or j],
    key=lambda s: -(min(s[0], 4 - s[0]) + min(s[1], 4 - s[1])),
)


def dot(a, b):
    return jnp.dot(a, b, preferred_element_type=F32)


def dot_nt(a, b):
    return lax.dot_general(a, b, (((1,), (1,)), ((), ())), preferred_element_type=F32)


def dot_tn(a, b):
    return lax.dot_general(a, b, (((0,), (0,)), ((), ())), preferred_element_type=F32)


def blocks(v):
    return jnp.concatenate(
        [v[:, k : k + 128] for k in range(0, v.shape[1], 128)], axis=0
    )


def unblocks(v):
    n = v.shape[0] * 8
    return jnp.concatenate(
        [v[:, k : k + 8].reshape(n, 128) for k in range(0, v.shape[1], 8)], axis=1
    )


def head_mask():
    lane = lax.broadcasted_iota(jnp.int32, (HEADS, HALF), 1)
    head = lax.broadcasted_iota(jnp.int32, (HEADS, HALF), 0) * HEAD_DIM
    return (lane >= head) & (lane < head + HEAD_DIM)


def expand_heads(v, mask):
    return jnp.concatenate(
        [jnp.where(mask, v[b : b + 1], 0.0) for b in range(GROUP)], axis=0
    ).astype(BF16)


def collapse_heads(v, mask):
    return jnp.concatenate(
        [
            jnp.sum(
                jnp.where(mask, v[b * HEADS : (b + 1) * HEADS], 0.0), axis=0, keepdims=True
            )
            for b in range(GROUP)
        ],
        axis=0,
    )


def row_sum(v):
    return jnp.sum(v, axis=-1, keepdims=True)


def kernel(
    x_hbm, wqkv_hbm, wout_hbm, wproj_hbm, other_hbm,
    loss_ref, gtok_ref, gqkv_ref, gout_ref, gproj_ref, gother_ref,
    other_ref, pairs_ref, x_ref, value_ref, wq_ref, wp0_ref, wp1_ref, wo_ref, wv_ref, wk_ref,
    xn_ref, mu_ref, inv_ref, grad_ref, dn_ref, dn0_ref, unit_ref, qbd_ref, dbd_ref, hn_ref, dhid_ref,
    s_cls, d_cls, s_oth, d_oth, s_q, d_q, s_kq, d_kq, s_w, d_w, s_ctx, d_ctx, s_att, d_att,
    s_u, d_u, s_cg, d_cg, s_sc, d_sc, s_kv, d_kv,
    f_oth, g_oth, f_emb, g_emb, f_a, g_a, f_b, g_b, f_c, g_c,
    load_sem, y_send, y_recv, b_send, b_recv, a_send, a_recv, core_send, core_recv,
    mod_send, mod_recv, all_send, all_recv, tp_send, tp_recv, dp_send, dp_recv,
):
    m, d, t = lax.axis_index("mod"), lax.axis_index("dp"), lax.axis_index("tp")
    me = t * N_MOD + m
    cx, cz = d // 4, lax.rem(d, 4)
    across = lax.rem(m + 2, N_MOD)
    sibling = m + 1 - 2 * lax.rem(m, 2)

    barrier = pltpu.get_barrier_semaphore()
    for k in range(1, N_MOD):
        pl.semaphore_signal(
            barrier, 1, device_id=(lax.rem(m + k, N_MOD), d, t), device_id_type=MESH
        )
    for k in range(N_MOD):
        pl.semaphore_signal(
            barrier, 1, device_id=(lax.rem(m + k, N_MOD), d, 1 - t), device_id_type=MESH
        )

    def greet(k, carry):
        pl.semaphore_signal(
            barrier, 1, device_id=(m, lax.rem(d + k, N_DP), t), device_id_type=MESH
        )
        return carry

    lax.fori_loop(1, N_DP, greet, 0)

    sources = (
        wproj_hbm.at[:, pl.ds(0, 512)], wproj_hbm.at[:, pl.ds(512, 512)], wout_hbm,
        wqkv_hbm.at[2], wqkv_hbm.at[1],
    )
    gathered = (wp0_ref, wp1_ref, wo_ref, wv_ref, wk_ref)
    load_x = pltpu.make_async_copy(x_hbm, pairs_ref, load_sem.at[6])
    load_x.start()
    load_other = pltpu.make_async_copy(other_hbm, other_ref, load_sem.at[7])
    load_other.start()
    load_q = pltpu.make_async_copy(wqkv_hbm.at[0], wq_ref, load_sem.at[5])
    load_q.start()
    loads = [
        pltpu.make_async_copy(src, dst.at[m], load_sem.at[i])
        for i, (src, dst) in enumerate(zip(sources, gathered))
    ]
    for i in (4, 3, 2, 0, 1):
        loads[i].start()

    leaving = []

    def remote(src, dst, send, recv, peer):
        return pltpu.make_async_remote_copy(
            src, dst, send, recv, device_id=peer, device_id_type=MESH
        )

    def start(copy):
        copy.start()

    def go(copy):
        copy.start()
        leaving.append(copy.wait_send)

    def rows_of(i, step):
        c = cx if ROWS_BY_X[i] else cz
        return pl.ds(pl.multiple_of(lax.rem(c + step, 4) * PIECE, 16), PIECE)

    def cols_of(i, step):
        c = cz if ROWS_BY_X[i] else cx
        return pl.ds(pl.multiple_of(lax.rem(c + step, 4) * 128, 128), 128)

    def row_peer(i, step):
        along_x = (m, lax.rem(cx + step, 4) * 4 + cz, t)
        along_z = (m, cx * 4 + lax.rem(cz + step, 4), t)
        return along_x if ROWS_BY_X[i] else along_z

    def col_peer(i, step):
        along_x = (m, lax.rem(cx + step, 4) * 4 + cz, t)
        along_z = (m, cx * 4 + lax.rem(cz + step, 4), t)
        return along_z if ROWS_BY_X[i] else along_x

    def pieces(i):
        yield 0, cols_of(i, 0)
        if COLUMNS[i] == 640:
            yield 1, pl.ds(512, 128)

    def fetch_core(i):
        go(remote(
            sources[i], gathered[i].at[m], core_send.at[i, 0], core_recv.at[i, 0], (sibling, d, t)
        ))

    def fetch_across(i):
        for n, cols in pieces(i):
            go(remote(
                sources[i].at[rows_of(i, 0), cols], gathered[i].at[m, rows_of(i, 0), cols],
                y_send.at[i, n], y_recv.at[i, n], (across, d, t),
            ))

    def share_cols(i):
        for n, cols in pieces(i):
            part_ref = gathered[i].at[across, rows_of(i, 0), cols]
            remote(
                part_ref, part_ref, y_send.at[i, n], y_recv.at[i, n], (across, d, t)
            ).wait_recv()
        part_ref = gathered[i].at[across, rows_of(i, 0), cols_of(i, 0)]
        for k in (2, 1, 3):
            start(remote(part_ref, part_ref, b_send.at[i], b_recv.at[i], col_peer(i, k)))
        three = gathered[i].at[across, pl.ds(0, PIECE), pl.ds(0, 384)]
        leaving.append(
            remote(three, three, b_send.at[i], b_recv.at[i], col_peer(i, 1)).wait_send
        )

    def share_rows(i):
        three = gathered[i].at[across, pl.ds(0, PIECE), pl.ds(0, 384)]
        remote(three, three, b_send.at[i], b_recv.at[i], col_peer(i, 1)).wait_recv()
        part_ref = gathered[i].at[across, rows_of(i, 0)]
        for k in (2, 1, 3):
            start(remote(part_ref, part_ref, a_send.at[i], a_recv.at[i], row_peer(i, k)))
        three = gathered[i].at[across, pl.ds(0, 3 * PIECE)]
        leaving.append(
            remote(three, three, a_send.at[i], a_recv.at[i], row_peer(i, 1)).wait_send
        )

    def share_core(i):
        three = gathered[i].at[across, pl.ds(0, 3 * PIECE)]
        remote(three, three, a_send.at[i], a_recv.at[i], row_peer(i, 1)).wait_recv()
        block = gathered[i].at[across]
        go(remote(block, block, core_send.at[i, 1], core_recv.at[i, 1], (sibling, d, t)))

    def complete(i):
        for n, owner in ((0, sibling), (1, lax.rem(sibling + 2, N_MOD))):
            block = gathered[i].at[owner]
            remote(
                block, block, core_send.at[i, n], core_recv.at[i, n], (sibling, d, t)
            ).wait_recv()

    def arrivals(dst, count, send, recv, peer):
        ref = dst.at[pl.ds(0, count)]
        return remote(ref, ref, send, recv, peer)

    def mod_all(n, dst):
        return arrivals(dst, N_MOD - 1, mod_send.at[n], mod_recv.at[n], (sibling, d, t))

    def mod_start(n, src, dst):
        for k in (2, 1, 3):
            peer = lax.rem(m + k, N_MOD)
            start(remote(src(peer), dst.at[m], mod_send.at[n], mod_recv.at[n], (peer, d, t)))
        leaving.append(lambda: mod_all(n, dst).wait_send())

    def mod_wait(n, dst):
        mod_all(n, dst).wait_recv()

    def all_all(n, dst):
        return arrivals(dst, 2 * N_MOD - 1, all_send.at[n], all_recv.at[n], (sibling, d, t))

    def all_start(n, src, dst):
        for k in range(2 * N_MOD - 1, 0, -1):
            peer = (lax.rem(m + k, N_MOD), d, t if k < N_MOD else 1 - t)
            start(remote(src, dst.at[me], all_send.at[n], all_recv.at[n], peer))
        leaving.append(lambda: all_all(n, dst).wait_send())

    def all_wait(n, dst):
        all_all(n, dst).wait_recv()

    def dp_all(n, dst):
        return arrivals(
            dst, N_DP - 1, dp_send.at[n], dp_recv.at[n], (m, lax.rem(d + 1, N_DP), t)
        )

    def dp_start(n, src, dst):
        def body(k, carry):
            peer = lax.rem(d + k, N_DP)
            start(remote(src(peer), dst.at[d], dp_send.at[n], dp_recv.at[n], (m, peer, t)))
            return carry

        lax.fori_loop(1, N_DP, body, 0)
        leaving.append(lambda: dp_all(n, dst).wait_send())

    def dp_start_far(n, src, dst):
        for i, j in FAR_FIRST:
            peer = lax.rem(cx + i, 4) * 4 + lax.rem(cz + j, 4)
            start(remote(src(peer), dst.at[d], dp_send.at[n], dp_recv.at[n], (m, peer, t)))
        leaving.append(lambda: dp_all(n, dst).wait_send())

    def dp_wait(n, dst):
        dp_all(n, dst).wait_recv()

    def tp_copy(n, src, dst):
        return remote(src, dst, tp_send.at[n], tp_recv.at[n], (m, d, 1 - t))

    def whole(ref):
        return lambda peer: ref

    def part(ref):
        return lambda peer: ref.at[peer]

    row8 = lax.broadcasted_iota(jnp.int32, (GROUP, 1), 0)
    mask = head_mask()

    def place(v):
        return jnp.where(row8 == 2 * m, v[0:1], jnp.where(row8 == 2 * m + 1, v[1:2], 0.0))

    def own_rows(v):
        first = jnp.sum(jnp.where(row8 == 2 * m, v, 0.0), axis=0, keepdims=True)
        second = jnp.sum(jnp.where(row8 == 2 * m + 1, v, 0.0), axis=0, keepdims=True)
        return jnp.where(row8 == 0, first, jnp.where(row8 == 1, second, 0.0))

    def normalise(c):
        at = pl.ds(c * CHUNK, CHUNK)
        x = x_ref[at, :].astype(F32)
        mu = row_sum(x) * (1.0 / D)
        x = x - mu
        inv = lax.rsqrt(row_sum(x * x) * (1.0 / D) + EPSILON)
        xn_ref[at, :] = (x * inv).astype(BF16)
        mu_ref[at, :] = mu
        inv_ref[at, :] = inv

    def window(v, k):
        wide = jnp.concatenate([v, jnp.zeros((v.shape[0], 192), F32)], axis=1)
        return wide[:, k * OUT_ROWS : k * OUT_ROWS + 128]

    def folded(v, k):
        wide = jnp.concatenate([v, jnp.zeros((64, 64), F32)], axis=1)
        at = k * OUT_ROWS
        return jnp.concatenate([wide[r : r + 16, at : at + 32] for r in range(0, 64, 16)], axis=1)

    def spread(dst, k, v):
        v = expand_heads(v, mask)
        at = pl.ds(pl.multiple_of(k * 16, 16), 16)
        for r in range(4):
            dst[r, at, :] = v[r * 16 : (r + 1) * 16]

    def head_grad(factor, dst):
        factor = factor.reshape(N_DP * 16, 128)
        return sum(
            dot_tn(factor, dst[r])[r * 32 : r * 32 + OUT_ROWS] for r in range(4)
        )

    def columns(v):
        return [v[:, p * SLICE : (p + 1) * SLICE] for p in range(N_MOD)]

    def full(ref):
        return ref[...].reshape(D, ref.shape[2])

    load_other.wait()
    load_x.wait()
    x8 = pairs_ref[0].astype(F32)
    mu8 = row_sum(x8) * (1.0 / D)
    c8 = x8 - mu8
    n8 = c8 * lax.rsqrt(row_sum(c8 * c8) * (1.0 / D) + EPSILON)
    for p, v in enumerate(columns(jnp.concatenate([place(n8), place(x8)], axis=0))):
        s_cls[p] = v.astype(BF16)
    d_cls[m] = s_cls[m]
    oth = blocks(place(other_ref[...].astype(F32))).astype(BF16)
    s_oth[...] = oth
    d_oth[m] = oth
    pl.semaphore_wait(barrier, N_MOD - 1 + N_MOD + N_DP - 1)
    mod_start(0, part(s_cls), d_cls)
    for i in range(5):
        fetch_across(i)
    for i in (0, 1):
        fetch_core(i)

    def interleave(k, carry):
        rows = pairs_ref[pl.ds(k * 16, 16)].astype(F32).reshape(32, D)
        x_ref[pl.ds(pl.multiple_of(k * 32, 32), 32), :] = rows.astype(BF16)
        return carry

    lax.fori_loop(0, 16, interleave, 0)
    last = jnp.concatenate([pairs_ref[TOK - 1].astype(F32), jnp.zeros((14, D), F32)], axis=0)
    x_ref[512:PAD_ROWS, :] = last.astype(BF16)
    normalise(0)
    load_q.wait()
    mod_wait(0, d_cls)
    cls = sum(d_cls[p].astype(F32) for p in range(N_MOD))
    n0, x0 = cls[0:8], cls[8:16]

    qp = dot(n0.astype(BF16), wq_ref[...])
    s_q[...] = qp
    d_q[m] = qp
    mod_start(1, whole(s_q), d_q)
    for i in (0, 1):
        share_cols(i)
    normalise(1)
    for i in (2, 3, 4):
        share_cols(i)
    loads[4].wait()
    mod_wait(1, d_q)
    q = (d_q[0] + d_q[1] + d_q[2] + d_q[3]).astype(BF16).astype(F32)

    kq = dot_nt(expand_heads(q, mask), wk_ref[m])
    for p in range(N_MOD):
        s_kq[p] = kq[p * 16 : (p + 1) * 16].astype(BF16)
    d_kq[m] = s_kq[m]
    mod_start(3, part(s_kq), d_kq)
    mod_start(2, whole(s_oth), d_oth)
    for i in (2, 3, 4):
        fetch_core(i)
    normalise(2)
    for i in range(5):
        share_rows(i)
    mod_wait(3, d_kq)
    kq_b = jnp.concatenate([d_kq[p].astype(F32) for p in range(N_MOD)], axis=1).astype(BF16)

    scores = dot_nt(kq_b, xn_ref[...]) * SCALE
    lane = lax.broadcasted_iota(jnp.int32, (16, PAD_ROWS), 1)
    image = lax.broadcasted_iota(jnp.int32, (16, PAD_ROWS), 0) >= HEADS
    valid = (((lane & 1) == 1) == image) & (lane < ROWS)
    expo = jnp.where(valid, jnp.exp(scores), 0.0)
    soft = expo / row_sum(expo)
    soft_b = soft.astype(BF16)
    w = dot(soft_b, xn_ref[...])
    for p, v in enumerate(columns(w)):
        s_w[p] = v.astype(BF16)
    d_w[m] = s_w[m]
    mod_start(4, part(s_w), d_w)
    mod_wait(2, d_oth)
    oth = d_oth[0].astype(F32) + d_oth[1].astype(F32)
    oth = (oth + d_oth[2].astype(F32) + d_oth[3].astype(F32)).astype(BF16)
    f_oth[...] = oth
    g_oth[d] = oth
    loads[3].wait()
    mod_wait(4, d_w)
    w64 = d_w[...].astype(F32).reshape(64, SLICE)

    cp = collapse_heads(dot(w64.astype(BF16), wv_ref[m]), mask)
    s_ctx[...] = cp
    d_ctx[m] = cp
    mod_start(5, whole(s_ctx), d_ctx)
    dp_start(0, whole(f_oth), g_oth)
    loads[2].wait()
    mod_wait(5, d_ctx)
    ctx = d_ctx[0] + d_ctx[1] + d_ctx[2] + d_ctx[3]

    ap = dot_nt(ctx.astype(BF16), wo_ref[m]) + jnp.where(t == 0, x0, 0.0)
    s_att[...] = ap
    d_att[me] = ap
    all_start(0, s_att, d_att)
    loads[0].wait()
    loads[1].wait()
    for i in (0, 1):
        share_core(i)
    all_wait(0, d_att)
    hid = [d_att[p] + d_att[p + N_MOD] for p in range(N_MOD)]
    hmu = sum(row_sum(h) for h in hid) * (1.0 / D)
    hvar = sum(row_sum((h - hmu) * (h - hmu)) for h in hid) * (1.0 / D)
    hinv = lax.rsqrt(hvar + EPSILON)
    for p in range(N_MOD):
        hn_ref[p] = (hid[p] - hmu) * hinv
    hn = jnp.concatenate([hn_ref[p] for p in range(N_MOD)], axis=1)

    hn_b = hn.astype(BF16)
    for i in (0, 1):
        complete(i)
    proj = jnp.concatenate([dot(hn_b, full(wp0_ref)), dot(hn_b, full(wp1_ref))], axis=1)
    pinv = lax.rsqrt(row_sum(proj * proj) + EPSILON)
    embed = proj * pinv
    emb = blocks(embed).astype(BF16)
    f_emb[...] = emb
    g_emb[d] = emb
    dp_start_far(1, whole(f_emb), g_emb)
    for i in (3, 2, 4):
        share_core(i)
    hn_m = hn_ref[m]
    common = jnp.concatenate([blocks(q), blocks(ctx)], axis=0)
    for k in range(N_DP):
        f_a[k] = jnp.concatenate(
            [folded(w64, k), window(n0, k), window(hn_m, k), common], axis=0
        ).astype(BF16)
    g_a[d] = f_a[d]
    dp_wait(0, g_oth)
    other_f = unblocks(g_oth[...].astype(F32))
    other_inv = lax.rsqrt(row_sum(other_f * other_f) + EPSILON)
    unit = other_f * other_inv
    unit_ref[...] = unit
    unit_b = unit.astype(BF16)
    dp_start(2, part(f_a), g_a)
    complete(3)
    for c in range(PAD_ROWS // CHUNK):
        at = pl.ds(c * CHUNK, CHUNK)
        value_ref[at, :] = dot(xn_ref[at, :], full(wv_ref)).astype(BF16)
    dp_wait(1, g_emb)

    emb_b = unblocks(g_emb[...].astype(F32)).astype(BF16)
    logits = dot_nt(emb_b, unit_b) * LOGIT_SCALE
    left = lax.broadcasted_iota(jnp.int32, (ALL, ALL), 0)
    right = lax.broadcasted_iota(jnp.int32, (ALL, ALL), 1)
    paired = ((left >> 1) & 3) == ((right >> 1) & 3)
    ex = jnp.where(paired, jnp.exp(logits), 0.0)
    row_total = row_sum(ex)
    col_total = jnp.sum(ex, axis=0, keepdims=True)
    grad = (0.5 / PAIRS) * (ex / row_total + ex / col_total)
    grad = grad - jnp.where(left == right, 1.0 / PAIRS, 0.0)
    grad_ref[...] = grad
    grad8 = grad_ref[pl.ds(d * GROUP, GROUP), :].astype(BF16)
    d_embed = LOGIT_SCALE * dot(grad8, unit_b)
    d_proj = (d_embed - embed * row_sum(embed * d_embed)) * pinv
    d_proj_b = d_proj.astype(BF16)
    dh = dot_nt(d_proj_b[:, :512], full(wp0_ref)) + dot_nt(d_proj_b[:, 512:], full(wp1_ref))
    m1 = row_sum(dh) * (1.0 / D)
    m2 = row_sum(dh * hn) * (1.0 / D)
    d_hidden = hinv * (dh - m1 - hn * m2)
    complete(2)
    d_context = dot(d_hidden.astype(BF16), full(wo_ref))

    mine = own_rows(d_context)
    heads = jnp.concatenate(
        [jnp.where(mask, mine[0:1], 0.0), jnp.where(mask, mine[1:2], 0.0)], axis=0
    ).astype(BF16)
    d_soft = dot_nt(heads, value_ref[...])
    d_score = soft * (d_soft - row_sum(soft * d_soft))
    d_score_b = d_score.astype(BF16)
    u = dot(d_score_b, xn_ref[...]) * SCALE
    complete(4)
    uk = dot(u.astype(BF16), full(wk_ref))
    dq = place(jnp.concatenate(
        [
            jnp.sum(jnp.where(mask, uk[0:8], 0.0), axis=0, keepdims=True),
            jnp.sum(jnp.where(mask, uk[8:16], 0.0), axis=0, keepdims=True),
        ],
        axis=0,
    ))
    dq = jnp.concatenate([dq[:, :SLICE], dq[:, SLICE:]], axis=0)
    for p, v in enumerate(columns(u)):
        s_u[p] = jnp.concatenate([v, dq], axis=0).astype(BF16)
    d_u[m] = s_u[m]
    mod_start(6, part(s_u), d_u)
    vd_b = dot_nt(heads, full(wv_ref)).astype(BF16)
    s_sc[0:16] = (d_score * SCALE).astype(BF16)
    s_sc[16:32] = soft_b
    s_kv[0:16] = kq_b
    s_kv[16:32] = vd_b
    go(tp_copy(0, s_sc, d_sc))
    go(tp_copy(1, s_kv, d_kv))
    for p, v in enumerate(columns(d_hidden)):
        dhid_ref[p] = v
    dhid_m = dhid_ref[m]
    high = pinv.astype(BF16).astype(F32)
    lane = lax.broadcasted_iota(jnp.int32, (GROUP, 128), 1)
    common = jnp.concatenate(
        [jnp.where(lane < 64, high, pinv - high), blocks(d_context), jnp.zeros((8, 128), F32)],
        axis=0,
    )
    for k in range(N_DP):
        f_b[k] = jnp.concatenate([window(dhid_m, k), common], axis=0).astype(BF16)
    g_b[d] = f_b[d]
    dp_start(3, part(f_b), g_b)
    mod_wait(6, d_u)
    ud = d_u[...].astype(F32)
    u64 = ud[:, 0:16].reshape(64, SLICE)
    dq = ud[0, 16:32] + ud[1, 16:32] + ud[2, 16:32] + ud[3, 16:32]
    dq = jnp.concatenate([dq[0:8], dq[8:16]], axis=1)
    common = jnp.concatenate([blocks(dq), jnp.zeros((8, 128), F32)], axis=0)
    for k in range(N_DP):
        f_c[k] = jnp.concatenate([folded(u64, k), common], axis=0).astype(BF16)
    g_c[d] = f_c[d]
    dp_start_far(4, part(f_c), g_c)
    cg = dot_nt(dq.astype(BF16), wq_ref[...])
    s_cg[...] = cg
    d_cg[me] = cg
    all_start(1, s_cg, d_cg)

    rows_m = ((lax.broadcasted_iota(jnp.int32, (ALL, 1), 0) >> 1) & 3) == m
    cols_m = ((lax.broadcasted_iota(jnp.int32, (1, ALL), 1) >> 1) & 3) == m
    diag = row_sum(jnp.where(left == right, logits, 0.0))
    loss = jnp.sum(
        jnp.where(rows_m, 0.5 * jnp.log(row_total) - diag, 0.0), axis=0, keepdims=True
    ) + row_sum(jnp.where(cols_m, 0.5 * jnp.log(col_total), 0.0))
    loss_ref[...] = jnp.broadcast_to(loss * (1.0 / PAIRS), (8, 128))
    d_unit = LOGIT_SCALE * dot_tn(grad.astype(BF16), emb_b)
    unit_ref[...] = (d_unit - unit * row_sum(unit * d_unit)) * other_inv
    gother_ref[...] = own_rows(unit_ref[pl.ds(d * GROUP, GROUP), :])[0:IMGS].astype(BF16)

    def spread_q(k, carry):
        spread(qbd_ref, k, unblocks(g_a[pl.ds(k, 1), 32:72].astype(F32)))
        return carry

    dp_wait(2, g_a)
    lax.fori_loop(0, N_DP, spread_q, 0)

    tp_copy(0, s_sc, d_sc).wait_recv()
    tp_copy(1, s_kv, d_kv).wait_recv()
    weights = jnp.concatenate([s_sc[...], d_sc[...]], axis=0).astype(F32).T.astype(BF16)
    factors = jnp.concatenate([s_kv[...], d_kv[...]], axis=0)
    half = pl.ds(pl.multiple_of(t * HALF, 128), HALF)
    for c in range(PAD_ROWS // CHUNK):
        at = pl.ds(c * CHUNK, CHUNK)
        dn = dot(weights[c * CHUNK : (c + 1) * CHUNK], factors)
        mu, inv = mu_ref[at, :], inv_ref[at, :]
        xh = (x_ref[at, :].astype(F32) - mu) * inv
        mean_grad = row_sum(dn) * (1.0 / D)
        mean_cross = row_sum(dn * xh) * (1.0 / D)
        dn_ref[...] = dn
        if c == 0:
            dn0_ref[...] = dn[0:8]
        xh = (x_ref[at, half].astype(F32) - mu) * inv
        grad_x = inv * (dn_ref[:, half] - mean_grad - xh * mean_cross)
        gtok_ref[pl.ds(c * CHUNK // 2, CHUNK // 2)] = grad_x.reshape(CHUNK // 2, IMGS, HALF).astype(
            BF16
        )

    all_wait(1, d_cg)
    extra = own_rows(
        jnp.concatenate([d_cg[p] + d_cg[p + N_MOD] for p in range(N_MOD)], axis=1)
    )
    dn = dn0_ref[...] + extra
    mu, inv = mu_ref[0:8, :], inv_ref[0:8, :]
    xh = (x_ref[0:16, :].astype(F32)[0:8] - mu) * inv
    mean_grad = row_sum(dn) * (1.0 / D)
    mean_cross = row_sum(dn * xh) * (1.0 / D)
    dn0_ref[...] = inv * (dn - mean_grad - xh * mean_cross) + own_rows(d_hidden)
    gtok_ref[0] = dn0_ref[:, half][0:IMGS].astype(BF16)

    def spread_c(k, carry):
        spread(dbd_ref, k, unblocks(g_b[pl.ds(k, 1), 16:56].astype(F32)))
        return carry

    dp_wait(3, g_b)
    lax.fori_loop(0, N_DP, spread_c, 0)
    gqkv_ref[2] = head_grad(g_a[:, 0:16], dbd_ref)
    early = g_a[...].astype(F32)
    late = g_b[...].astype(F32)
    dhid_all = unblocks(late[:, 0:8]).astype(BF16)
    gout_ref[...] = dot_tn(dhid_all, unblocks(early[:, 72:112]).astype(BF16))[0:OUT_ROWS]
    pinv_all = unblocks(late[:, 8:16])
    pinv_all = pinv_all[:, 0:1] + pinv_all[:, 64:65]
    emb = emb_b.astype(F32)
    d_embed = LOGIT_SCALE * dot(grad.astype(BF16), unit_b)
    d_proj = (d_embed - emb * row_sum(emb * d_embed)) * pinv_all
    hn_all = unblocks(early[:, 24:32]).astype(BF16)
    gproj_ref[...] = dot_tn(hn_all, d_proj.astype(BF16))[0:OUT_ROWS]
    n0_all = unblocks(early[:, 16:24]).astype(BF16)
    dp_wait(4, g_c)
    gqkv_ref[1] = head_grad(g_c[:, 0:16], qbd_ref)
    dq_all = unblocks(g_c[...].astype(F32)[:, 16:56]).astype(BF16)
    gqkv_ref[0] = dot_tn(n0_all, dq_all)[0:OUT_ROWS]

    for wait in leaving:
        wait()


def store(*refs):
    sources, targets, sem = refs[:6], refs[6:12], refs[12]
    copies = [
        pltpu.make_async_copy(src, dst, sem.at[k])
        for k, (src, dst) in enumerate(
            [(sources[1].at[pl.ds(0, TOK)], targets[1])] + list(zip(sources[2:], targets[2:]))
        )
    ]
    for copy in copies:
        copy.start()
    targets[0][0] = jnp.max(sources[0][0:1, 0:1])
    for copy in copies:
        copy.wait()


def local(tokens, w_qkv, w_out, w_proj, other_emb):
    vmem = pl.BlockSpec(memory_space=pltpu.VMEM)
    hbm = pl.BlockSpec(memory_space=pltpu.HBM)

    def pair(send, land, dtype=F32):
        return [pltpu.VMEM(send, dtype), pltpu.VMEM(land, dtype)]

    def mod_all(n, k):
        return pair((n, k), (N_MOD, n, k))

    def mod_each(n):
        return pair((N_MOD, n, SLICE), (N_MOD, n, SLICE), BF16)

    def dp_all(n):
        return pair((n, 128), (N_DP, n, 128), BF16)

    def dp_each(n):
        return pair((N_DP, n, 128), (N_DP, n, 128), BF16)

    scratch = [pltpu.VMEM((IMGS, E), BF16), pltpu.VMEM((TOK, IMGS, D), BF16), pltpu.VMEM((PAD_ROWS, D), BF16)]
    scratch += [pltpu.VMEM((PAD_ROWS, HALF), BF16)]
    scratch += [pltpu.VMEM((SLICE, HALF), BF16)]
    scratch += [pltpu.VMEM((N_MOD, SLICE, k), BF16) for k in COLUMNS]
    scratch += [
        pltpu.VMEM((PAD_ROWS, D), BF16),
        pltpu.VMEM((PAD_ROWS, 1), F32),
        pltpu.VMEM((PAD_ROWS, 1), F32),
        pltpu.VMEM((ALL, ALL), F32),
        pltpu.VMEM((CHUNK, D), F32),
        pltpu.VMEM((8, D), F32),
        pltpu.VMEM((ALL, E), F32),
        pltpu.VMEM((4, N_DP * 16, HALF), BF16),
        pltpu.VMEM((4, N_DP * 16, HALF), BF16),
        pltpu.VMEM((N_MOD, GROUP, SLICE), F32),
        pltpu.VMEM((N_MOD, GROUP, SLICE), F32),
    ]
    scratch += mod_each(16) + pair((64, 128), (N_MOD, 64, 128), BF16) + mod_all(8, HALF) + mod_each(16) + mod_each(16)
    scratch += mod_all(8, HALF) + pair((8, SLICE), (2 * N_MOD, 8, SLICE))
    scratch += mod_each(32) + pair((8, SLICE), (2 * N_MOD, 8, SLICE))
    scratch += pair((32, PAD_ROWS), (32, PAD_ROWS), BF16) + pair((32, D), (32, D), BF16)
    scratch += dp_all(64) + dp_all(64) + dp_each(112) + dp_each(64) + dp_each(64)
    dma = pltpu.SemaphoreType.DMA
    n = len(COLUMNS)
    scratch += [dma((n + 3,)), dma((n, 2)), dma((n, 2)), dma((n,)), dma((n,))]
    scratch += [dma((n,)), dma((n,)), dma((n, 2)), dma((n, 2))]
    scratch += [dma((7,)), dma((7,)), dma((2,)), dma((2,)), dma((2,)), dma((2,))]
    scratch += [dma((5,)), dma((5,))]

    def shape(*dims, dtype=F32):
        return jax.ShapeDtypeStruct(dims, dtype)

    results = pl.pallas_call(
        kernel,
        out_shape=[
            shape(8, 128),
            shape(PAD_TOK, IMGS, HALF, dtype=BF16),
            shape(3, OUT_ROWS, HALF),
            shape(OUT_ROWS, HALF),
            shape(OUT_ROWS, E),
            shape(IMGS, E, dtype=BF16),
        ],
        in_specs=[hbm] * 5,
        out_specs=[vmem] * 6,
        scratch_shapes=scratch,
        compiler_params=pltpu.CompilerParams(
            collective_id=0, has_side_effects=True, vmem_limit_bytes=48 * 2**20
        ),
    )(
        *(
            pltpu.with_memory_space_constraint(v, pltpu.HBM)
            for v in (
                tokens.transpose(1, 0, 2), w_qkv.transpose(1, 0, 2), w_out, w_proj, other_emb
            )
        )
    )
    loss, grad_tokens, grad_qkv, grad_out, grad_proj, grad_other = pl.pallas_call(
        store,
        out_shape=[
            shape(1),
            shape(TOK, IMGS, HALF, dtype=BF16),
            shape(3, OUT_ROWS, HALF),
            shape(OUT_ROWS, HALF),
            shape(OUT_ROWS, E),
            shape(IMGS, E, dtype=BF16),
        ],
        in_specs=[vmem] * 6,
        out_specs=[pl.BlockSpec(memory_space=pltpu.SMEM)] + [hbm] * 5,
        scratch_shapes=[pltpu.SemaphoreType.DMA((5,))],
        compiler_params=pltpu.CompilerParams(vmem_limit_bytes=16 * 2**20),
    )(*results)
    return (
        loss,
        grad_tokens.transpose(1, 0, 2),
        grad_qkv.transpose(1, 0, 2),
        grad_out,
        grad_proj,
        grad_other,
    )


def solution(mesh):
    placed = (
        P(("mod", "dp"), None, None),
        P("mod", None, "tp"),
        P("mod", "tp"),
        P("mod", None),
        P(("mod", "dp"), None),
    )
    return jax.shard_map(
        local,
        mesh=mesh,
        in_specs=placed,
        out_specs=(
            P("mod"),
            P(("mod", "dp"), None, "tp"),
            P(("mod", "dp"), None, "tp"),
            P(("mod", "dp"), "tp"),
            P(("mod", "dp"), None),
            P(("mod", "dp"), None),
        ),
        check_vma=False,
    )
```

```python
import functools

import jax
import jax.numpy as jnp
from jax import lax
from jax.experimental import pallas as pl
from jax.experimental.pallas import tpu as pltpu
from jax.sharding import PartitionSpec as P

HEAD_DIM = 80
EPSILON = 1e-06
LOGIT_SCALE = 1.0 / 0.07
MESH = pl.DeviceIdType.MESH
F32 = jnp.float32
BF16 = jnp.bfloat16

N_MOD, N_DP, N_TP = 4, 16, 2
IMGS = 2
GROUP = N_MOD * IMGS
HEADS = 8
TOK = 257
ROWS = IMGS * TOK
PAD_ROWS = 528
PAD_TOK = PAD_ROWS // IMGS
CHUNK = 176
D = 1280
HALF = D // 2
SLICE = D // N_MOD
OUT_ROWS = SLICE // N_DP
E = 1024
PAIRS = 32
ALL = GROUP * N_DP
SCALE = HEAD_DIM**-0.5
COLUMNS = (512, 512, 640, 640, 640)
ROWS_BY_X = (True, False, True, False, True)
PIECE = SLICE // 4
FAR_FIRST = sorted(
    [(i, j) for i in range(4) for j in range(4) if i or j],
    key=lambda s: -(min(s[0], 4 - s[0]) + min(s[1], 4 - s[1])),
)


def dot(a, b):
    return jnp.dot(a, b, preferred_element_type=F32)


def dot_nt(a, b):
    return lax.dot_general(a, b, (((1,), (1,)), ((), ())), preferred_element_type=F32)


def dot_tn(a, b):
    return lax.dot_general(a, b, (((0,), (0,)), ((), ())), preferred_element_type=F32)


def blocks(v):
    return jnp.concatenate(
        [v[:, k : k + 128] for k in range(0, v.shape[1], 128)], axis=0
    )


def unblocks(v):
    n = v.shape[0] * 8
    return jnp.concatenate(
        [v[:, k : k + 8].reshape(n, 128) for k in range(0, v.shape[1], 8)], axis=1
    )


def head_mask():
    lane = lax.broadcasted_iota(jnp.int32, (HEADS, HALF), 1)
    head = lax.broadcasted_iota(jnp.int32, (HEADS, HALF), 0) * HEAD_DIM
    return (lane >= head) & (lane < head + HEAD_DIM)


def expand_heads(v, mask):
    return jnp.concatenate(
        [jnp.where(mask, v[b : b + 1], 0.0) for b in range(GROUP)], axis=0
    ).astype(BF16)


def collapse_heads(v, mask):
    return jnp.concatenate(
        [
            jnp.sum(
                jnp.where(mask, v[b * HEADS : (b + 1) * HEADS], 0.0), axis=0, keepdims=True
            )
            for b in range(GROUP)
        ],
        axis=0,
    )


def row_sum(v):
    return jnp.sum(v, axis=-1, keepdims=True)


def kernel(
    x_hbm, wqkv_hbm, wout_hbm, wproj_hbm, other_hbm,
    loss_ref, gtok_ref, gqkv_ref, gout_ref, gproj_ref, gother_ref,
    other_ref, pairs_ref, x_ref, value_ref, wq_ref, wp0_ref, wp1_ref, wo_ref, wv_ref, wk_ref,
    xn_ref, mu_ref, inv_ref, grad_ref, dn_ref, dn0_ref, unit_ref, qbd_ref, dbd_ref, hn_ref, dhid_ref,
    s_cls, d_cls, s_oth, d_oth, s_q, d_q, s_kq, d_kq, s_w, d_w, s_ctx, d_ctx, s_att, d_att,
    s_u, d_u, s_cg, d_cg, s_sc, d_sc, s_kv, d_kv,
    f_oth, g_oth, f_emb, g_emb, f_a, g_a, f_b, g_b, f_c, g_c,
    load_sem, y_send, y_recv, b_send, b_recv, a_send, a_recv, core_send, core_recv,
    mod_send, mod_recv, all_send, all_recv, tp_send, tp_recv, dp_send, dp_recv,
):
    m, d, t = lax.axis_index("mod"), lax.axis_index("dp"), lax.axis_index("tp")
    me = t * N_MOD + m
    cx, cz = d // 4, lax.rem(d, 4)
    across = lax.rem(m + 2, N_MOD)
    sibling = m + 1 - 2 * lax.rem(m, 2)

    barrier = pltpu.get_barrier_semaphore()
    for k in range(1, N_MOD):
        pl.semaphore_signal(
            barrier, 1, device_id=(lax.rem(m + k, N_MOD), d, t), device_id_type=MESH
        )
    for k in range(N_MOD):
        pl.semaphore_signal(
            barrier, 1, device_id=(lax.rem(m + k, N_MOD), d, 1 - t), device_id_type=MESH
        )

    def greet(k, carry):
        pl.semaphore_signal(
            barrier, 1, device_id=(m, lax.rem(d + k, N_DP), t), device_id_type=MESH
        )
        return carry

    lax.fori_loop(1, N_DP, greet, 0)

    sources = (
        wproj_hbm.at[:, pl.ds(0, 512)], wproj_hbm.at[:, pl.ds(512, 512)], wout_hbm,
        wqkv_hbm.at[2], wqkv_hbm.at[1],
    )
    gathered = (wp0_ref, wp1_ref, wo_ref, wv_ref, wk_ref)
    load_x = pltpu.make_async_copy(x_hbm, pairs_ref, load_sem.at[6])
    load_x.start()
    load_other = pltpu.make_async_copy(other_hbm, other_ref, load_sem.at[7])
    load_other.start()
    load_q = pltpu.make_async_copy(wqkv_hbm.at[0], wq_ref, load_sem.at[5])
    load_q.start()
    loads = [
        pltpu.make_async_copy(src, dst.at[m], load_sem.at[i])
        for i, (src, dst) in enumerate(zip(sources, gathered))
    ]
    for i in (4, 3, 2, 0, 1):
        loads[i].start()

    leaving = []

    def remote(src, dst, send, recv, peer):
        return pltpu.make_async_remote_copy(
            src, dst, send, recv, device_id=peer, device_id_type=MESH
        )

    def start(copy):
        copy.start()

    def go(copy):
        copy.start()
        leaving.append(copy.wait_send)

    def rows_of(i, step):
        c = cx if ROWS_BY_X[i] else cz
        return pl.ds(pl.multiple_of(lax.rem(c + step, 4) * PIECE, 16), PIECE)

    def cols_of(i, step):
        c = cz if ROWS_BY_X[i] else cx
        return pl.ds(pl.multiple_of(lax.rem(c + step, 4) * 128, 128), 128)

    def row_peer(i, step):
        along_x = (m, lax.rem(cx + step, 4) * 4 + cz, t)
        along_z = (m, cx * 4 + lax.rem(cz + step, 4), t)
        return along_x if ROWS_BY_X[i] else along_z

    def col_peer(i, step):
        along_x = (m, lax.rem(cx + step, 4) * 4 + cz, t)
        along_z = (m, cx * 4 + lax.rem(cz + step, 4), t)
        return along_z if ROWS_BY_X[i] else along_x

    def pieces(i):
        yield cols_of(i, 0)
        if COLUMNS[i] == 640:
            yield pl.ds(512, 128)

    def fetch_core(i):
        start(remote(
            sources[i], gathered[i].at[m], core_send.at[i], core_recv.at[i, 0], (sibling, d, t)
        ))

    def fetch_across(i):
        for cols in pieces(i):
            start(remote(
                sources[i].at[rows_of(i, 0), cols], gathered[i].at[m, rows_of(i, 0), cols],
                y_send, y_recv.at[i], (across, d, t),
            ))

    def share_cols(i):
        wide = 256 if COLUMNS[i] == 640 else 128
        landed = gathered[i].at[across, pl.ds(0, PIECE), pl.ds(0, wide)]
        remote(landed, landed, y_send, y_recv.at[i], (across, d, t)).wait_recv()
        part_ref = gathered[i].at[across, rows_of(i, 0), cols_of(i, 0)]
        for k in (2, 1, 3):
            start(remote(part_ref, part_ref, b_send, b_recv.at[i], col_peer(i, k)))

    def pieces_left():
        sent = wo_ref.at[across, pl.ds(0, 160), pl.ds(0, 512)]
        leaving.append(remote(sent, sent, y_send, y_recv.at[0], (across, d, t)).wait_send)
        sent = wo_ref.at[across, pl.ds(0, 240)]
        leaving.append(remote(sent, sent, b_send, b_recv.at[0], col_peer(0, 1)).wait_send)

    def share_rows(i):
        three = gathered[i].at[across, pl.ds(0, PIECE), pl.ds(0, 384)]
        remote(three, three, b_send, b_recv.at[i], col_peer(i, 1)).wait_recv()
        part_ref = gathered[i].at[across, rows_of(i, 0)]
        for k in (2, 1, 3):
            start(remote(part_ref, part_ref, a_send.at[i], a_recv.at[i], row_peer(i, k)))
        three = gathered[i].at[across, pl.ds(0, 3 * PIECE)]
        leaving.append(
            remote(three, three, a_send.at[i], a_recv.at[i], row_peer(i, 1)).wait_send
        )

    def share_core(i):
        three = gathered[i].at[across, pl.ds(0, 3 * PIECE)]
        remote(three, three, a_send.at[i], a_recv.at[i], row_peer(i, 1)).wait_recv()
        block = gathered[i].at[across]
        start(remote(block, block, core_send.at[i], core_recv.at[i, 1], (sibling, d, t)))
        two = gathered[i].at[pl.ds(0, 2)]
        leaving.append(
            remote(two, two, core_send.at[i], core_recv.at[i, 1], (sibling, d, t)).wait_send
        )

    def complete(i):
        for n, owner in ((0, sibling), (1, lax.rem(sibling + 2, N_MOD))):
            block = gathered[i].at[owner]
            remote(
                block, block, core_send.at[i], core_recv.at[i, n], (sibling, d, t)
            ).wait_recv()

    def arrivals(dst, count, send, recv, peer):
        ref = dst.at[pl.ds(0, count)]
        return remote(ref, ref, send, recv, peer)

    def mod_all(n, dst):
        return arrivals(dst, N_MOD - 1, mod_send.at[n], mod_recv.at[n], (sibling, d, t))

    def mod_start(n, src, dst):
        for k in (2, 1, 3):
            peer = lax.rem(m + k, N_MOD)
            start(remote(src(peer), dst.at[m], mod_send.at[n], mod_recv.at[n], (peer, d, t)))
        leaving.append(lambda: mod_all(n, dst).wait_send())

    def mod_wait(n, dst):
        mod_all(n, dst).wait_recv()

    def all_all(n, dst):
        return arrivals(dst, 2 * N_MOD - 1, all_send.at[n], all_recv.at[n], (sibling, d, t))

    def all_start(n, src, dst):
        for k in range(2 * N_MOD - 1, 0, -1):
            peer = (lax.rem(m + k, N_MOD), d, t if k < N_MOD else 1 - t)
            start(remote(src, dst.at[me], all_send.at[n], all_recv.at[n], peer))
        leaving.append(lambda: all_all(n, dst).wait_send())

    def all_wait(n, dst):
        all_all(n, dst).wait_recv()

    def dp_all(n, dst):
        return arrivals(
            dst, N_DP - 1, dp_send.at[n], dp_recv.at[n], (m, lax.rem(d + 1, N_DP), t)
        )

    def dp_start(n, src, dst):
        def body(k, carry):
            peer = lax.rem(d + k, N_DP)
            start(remote(src(peer), dst.at[d], dp_send.at[n], dp_recv.at[n], (m, peer, t)))
            return carry

        lax.fori_loop(1, N_DP, body, 0)
        leaving.append(lambda: dp_all(n, dst).wait_send())

    def dp_start_far(n, src, dst):
        for i, j in FAR_FIRST:
            peer = lax.rem(cx + i, 4) * 4 + lax.rem(cz + j, 4)
            start(remote(src(peer), dst.at[d], dp_send.at[n], dp_recv.at[n], (m, peer, t)))
        leaving.append(lambda: dp_all(n, dst).wait_send())

    def dp_wait(n, dst):
        dp_all(n, dst).wait_recv()

    def tp_copy(n, src, dst):
        return remote(src, dst, tp_send.at[n], tp_recv.at[n], (m, d, 1 - t))

    def whole(ref):
        return lambda peer: ref

    def part(ref):
        return lambda peer: ref.at[peer]

    row8 = lax.broadcasted_iota(jnp.int32, (GROUP, 1), 0)
    mask = head_mask()

    def place(v):
        return jnp.where(row8 == 2 * m, v[0:1], jnp.where(row8 == 2 * m + 1, v[1:2], 0.0))

    def own_rows(v):
        first = jnp.sum(jnp.where(row8 == 2 * m, v, 0.0), axis=0, keepdims=True)
        second = jnp.sum(jnp.where(row8 == 2 * m + 1, v, 0.0), axis=0, keepdims=True)
        return jnp.where(row8 == 0, first, jnp.where(row8 == 1, second, 0.0))

    def normalise(c):
        at = pl.ds(c * CHUNK, CHUNK)
        x = x_ref[at, :].astype(F32)
        mu = row_sum(x) * (1.0 / D)
        x = x - mu
        inv = lax.rsqrt(row_sum(x * x) * (1.0 / D) + EPSILON)
        xn_ref[at, :] = (x * inv).astype(BF16)
        mu_ref[at, :] = mu
        inv_ref[at, :] = inv

    def window(v, k):
        wide = jnp.concatenate([v, jnp.zeros((v.shape[0], 192), F32)], axis=1)
        return wide[:, k * OUT_ROWS : k * OUT_ROWS + 128]

    def folded(v, k):
        wide = jnp.concatenate([v, jnp.zeros((64, 64), F32)], axis=1)
        at = k * OUT_ROWS
        return jnp.concatenate([wide[r : r + 16, at : at + 32] for r in range(0, 64, 16)], axis=1)

    def spread(dst, k, v):
        v = expand_heads(v, mask)
        at = pl.ds(pl.multiple_of(k * 16, 16), 16)
        for r in range(4):
            dst[r, at, :] = v[r * 16 : (r + 1) * 16]

    def head_grad(factor, dst):
        factor = factor.reshape(N_DP * 16, 128)
        return sum(
            dot_tn(factor, dst[r])[r * 32 : r * 32 + OUT_ROWS] for r in range(4)
        )

    def columns(v):
        return [v[:, p * SLICE : (p + 1) * SLICE] for p in range(N_MOD)]

    def full(ref):
        return ref[...].reshape(D, ref.shape[2])

    load_other.wait()
    load_x.wait()
    x8 = pairs_ref[0].astype(F32)
    mu8 = row_sum(x8) * (1.0 / D)
    c8 = x8 - mu8
    n8 = c8 * lax.rsqrt(row_sum(c8 * c8) * (1.0 / D) + EPSILON)
    for p, v in enumerate(columns(jnp.concatenate([place(n8), place(x8)], axis=0))):
        s_cls[p] = v.astype(BF16)
    d_cls[m] = s_cls[m]
    oth = blocks(place(other_ref[...].astype(F32))).astype(BF16)
    s_oth[...] = oth
    d_oth[m] = oth
    pl.semaphore_wait(barrier, N_MOD - 1 + N_MOD + N_DP - 1)
    mod_start(0, part(s_cls), d_cls)
    for i in range(5):
        fetch_across(i)
    for i in (0, 1):
        fetch_core(i)

    def interleave(k, carry):
        rows = pairs_ref[pl.ds(k * 16, 16)].astype(F32).reshape(32, D)
        x_ref[pl.ds(pl.multiple_of(k * 32, 32), 32), :] = rows.astype(BF16)
        return carry

    lax.fori_loop(0, 16, interleave, 0)
    last = jnp.concatenate([pairs_ref[TOK - 1].astype(F32), jnp.zeros((14, D), F32)], axis=0)
    x_ref[512:PAD_ROWS, :] = last.astype(BF16)
    normalise(0)
    load_q.wait()
    mod_wait(0, d_cls)
    cls = sum(d_cls[p].astype(F32) for p in range(N_MOD))
    n0, x0 = cls[0:8], cls[8:16]

    qp = dot(n0.astype(BF16), wq_ref[...])
    s_q[...] = qp
    d_q[m] = qp
    mod_start(1, whole(s_q), d_q)
    for i in (0, 1):
        share_cols(i)
    normalise(1)
    for i in (2, 3, 4):
        share_cols(i)
    pieces_left()
    loads[4].wait()
    mod_wait(1, d_q)
    q = (d_q[0] + d_q[1] + d_q[2] + d_q[3]).astype(BF16).astype(F32)

    kq = dot_nt(expand_heads(q, mask), wk_ref[m])
    for p in range(N_MOD):
        s_kq[p] = kq[p * 16 : (p + 1) * 16].astype(BF16)
    d_kq[m] = s_kq[m]
    mod_start(3, part(s_kq), d_kq)
    mod_start(2, whole(s_oth), d_oth)
    for i in (2, 3, 4):
        fetch_core(i)
    normalise(2)
    for i in range(5):
        share_rows(i)
    mod_wait(3, d_kq)
    kq_b = jnp.concatenate([d_kq[p].astype(F32) for p in range(N_MOD)], axis=1).astype(BF16)

    scores = dot_nt(kq_b, xn_ref[...]) * SCALE
    lane = lax.broadcasted_iota(jnp.int32, (16, PAD_ROWS), 1)
    image = lax.broadcasted_iota(jnp.int32, (16, PAD_ROWS), 0) >= HEADS
    valid = (((lane & 1) == 1) == image) & (lane < ROWS)
    expo = jnp.where(valid, jnp.exp(scores), 0.0)
    soft = expo / row_sum(expo)
    soft_b = soft.astype(BF16)
    w = dot(soft_b, xn_ref[...])
    for p, v in enumerate(columns(w)):
        s_w[p] = v.astype(BF16)
    d_w[m] = s_w[m]
    mod_start(4, part(s_w), d_w)
    mod_wait(2, d_oth)
    oth = d_oth[0].astype(F32) + d_oth[1].astype(F32)
    oth = (oth + d_oth[2].astype(F32) + d_oth[3].astype(F32)).astype(BF16)
    f_oth[...] = oth
    g_oth[d] = oth
    loads[3].wait()
    mod_wait(4, d_w)
    w64 = d_w[...].astype(F32).reshape(64, SLICE)

    cp = collapse_heads(dot(w64.astype(BF16), wv_ref[m]), mask)
    s_ctx[...] = cp
    d_ctx[m] = cp
    mod_start(5, whole(s_ctx), d_ctx)
    dp_start(0, whole(f_oth), g_oth)
    loads[2].wait()
    mod_wait(5, d_ctx)
    ctx = d_ctx[0] + d_ctx[1] + d_ctx[2] + d_ctx[3]

    ap = dot_nt(ctx.astype(BF16), wo_ref[m]) + jnp.where(t == 0, x0, 0.0)
    s_att[...] = ap
    d_att[me] = ap
    all_start(0, s_att, d_att)
    loads[0].wait()
    loads[1].wait()
    for i in (0, 1):
        share_core(i)
    all_wait(0, d_att)
    hid = [d_att[p] + d_att[p + N_MOD] for p in range(N_MOD)]
    hmu = sum(row_sum(h) for h in hid) * (1.0 / D)
    hvar = sum(row_sum((h - hmu) * (h - hmu)) for h in hid) * (1.0 / D)
    hinv = lax.rsqrt(hvar + EPSILON)
    for p in range(N_MOD):
        hn_ref[p] = (hid[p] - hmu) * hinv
    hn = jnp.concatenate([hn_ref[p] for p in range(N_MOD)], axis=1)

    hn_b = hn.astype(BF16)
    for i in (0, 1):
        complete(i)
    proj = jnp.concatenate([dot(hn_b, full(wp0_ref)), dot(hn_b, full(wp1_ref))], axis=1)
    pinv = lax.rsqrt(row_sum(proj * proj) + EPSILON)
    embed = proj * pinv
    emb = blocks(embed).astype(BF16)
    f_emb[...] = emb
    g_emb[d] = emb
    dp_start_far(1, whole(f_emb), g_emb)
    for i in (3, 2, 4):
        share_core(i)
    hn_m = hn_ref[m]
    common = jnp.concatenate([blocks(q), blocks(ctx)], axis=0)
    for k in range(N_DP):
        f_a[k] = jnp.concatenate(
            [folded(w64, k), window(n0, k), window(hn_m, k), common], axis=0
        ).astype(BF16)
    g_a[d] = f_a[d]
    dp_wait(0, g_oth)
    other_f = unblocks(g_oth[...].astype(F32))
    other_inv = lax.rsqrt(row_sum(other_f * other_f) + EPSILON)
    unit = other_f * other_inv
    unit_ref[...] = unit
    unit_b = unit.astype(BF16)
    dp_start(2, part(f_a), g_a)
    complete(3)
    for c in range(PAD_ROWS // CHUNK):
        at = pl.ds(c * CHUNK, CHUNK)
        value_ref[at, :] = dot(xn_ref[at, :], full(wv_ref)).astype(BF16)
    dp_wait(1, g_emb)

    emb_b = unblocks(g_emb[...].astype(F32)).astype(BF16)
    logits = dot_nt(emb_b, unit_b) * LOGIT_SCALE
    left = lax.broadcasted_iota(jnp.int32, (ALL, ALL), 0)
    right = lax.broadcasted_iota(jnp.int32, (ALL, ALL), 1)
    paired = ((left >> 1) & 3) == ((right >> 1) & 3)
    ex = jnp.where(paired, jnp.exp(logits), 0.0)
    row_total = row_sum(ex)
    col_total = jnp.sum(ex, axis=0, keepdims=True)
    grad = (0.5 / PAIRS) * (ex / row_total + ex / col_total)
    grad = grad - jnp.where(left == right, 1.0 / PAIRS, 0.0)
    grad_ref[...] = grad
    grad8 = grad_ref[pl.ds(d * GROUP, GROUP), :].astype(BF16)
    d_embed = LOGIT_SCALE * dot(grad8, unit_b)
    d_proj = (d_embed - embed * row_sum(embed * d_embed)) * pinv
    d_proj_b = d_proj.astype(BF16)
    dh = dot_nt(d_proj_b[:, :512], full(wp0_ref)) + dot_nt(d_proj_b[:, 512:], full(wp1_ref))
    m1 = row_sum(dh) * (1.0 / D)
    m2 = row_sum(dh * hn) * (1.0 / D)
    d_hidden = hinv * (dh - m1 - hn * m2)
    complete(2)
    d_context = dot(d_hidden.astype(BF16), full(wo_ref))

    mine = own_rows(d_context)
    heads = jnp.concatenate(
        [jnp.where(mask, mine[0:1], 0.0), jnp.where(mask, mine[1:2], 0.0)], axis=0
    ).astype(BF16)
    d_soft = dot_nt(heads, value_ref[...])
    d_score = soft * (d_soft - row_sum(soft * d_soft))
    d_score_b = d_score.astype(BF16)
    u = dot(d_score_b, xn_ref[...]) * SCALE
    complete(4)
    uk = dot(u.astype(BF16), full(wk_ref))
    dq = place(jnp.concatenate(
        [
            jnp.sum(jnp.where(mask, uk[0:8], 0.0), axis=0, keepdims=True),
            jnp.sum(jnp.where(mask, uk[8:16], 0.0), axis=0, keepdims=True),
        ],
        axis=0,
    ))
    dq = jnp.concatenate([dq[:, :SLICE], dq[:, SLICE:]], axis=0)
    for p, v in enumerate(columns(u)):
        s_u[p] = jnp.concatenate([v, dq], axis=0).astype(BF16)
    d_u[m] = s_u[m]
    mod_start(6, part(s_u), d_u)
    vd_b = dot_nt(heads, full(wv_ref)).astype(BF16)
    s_sc[0:16] = (d_score * SCALE).astype(BF16)
    s_sc[16:32] = soft_b
    s_kv[0:16] = kq_b
    s_kv[16:32] = vd_b
    go(tp_copy(0, s_sc, d_sc))
    go(tp_copy(1, s_kv, d_kv))
    for p, v in enumerate(columns(d_hidden)):
        dhid_ref[p] = v
    dhid_m = dhid_ref[m]
    high = pinv.astype(BF16).astype(F32)
    lane = lax.broadcasted_iota(jnp.int32, (GROUP, 128), 1)
    common = jnp.concatenate(
        [jnp.where(lane < 64, high, pinv - high), blocks(d_context), jnp.zeros((8, 128), F32)],
        axis=0,
    )
    for k in range(N_DP):
        f_b[k] = jnp.concatenate([window(dhid_m, k), common], axis=0).astype(BF16)
    g_b[d] = f_b[d]
    dp_start(3, part(f_b), g_b)
    mod_wait(6, d_u)
    ud = d_u[...].astype(F32)
    u64 = ud[:, 0:16].reshape(64, SLICE)
    dq = ud[0, 16:32] + ud[1, 16:32] + ud[2, 16:32] + ud[3, 16:32]
    dq = jnp.concatenate([dq[0:8], dq[8:16]], axis=1)
    common = jnp.concatenate([blocks(dq), jnp.zeros((8, 128), F32)], axis=0)
    for k in range(N_DP):
        f_c[k] = jnp.concatenate([folded(u64, k), common], axis=0).astype(BF16)
    g_c[d] = f_c[d]
    dp_start_far(4, part(f_c), g_c)
    cg = dot_nt(dq.astype(BF16), wq_ref[...])
    s_cg[...] = cg
    d_cg[me] = cg
    all_start(1, s_cg, d_cg)

    rows_m = ((lax.broadcasted_iota(jnp.int32, (ALL, 1), 0) >> 1) & 3) == m
    cols_m = ((lax.broadcasted_iota(jnp.int32, (1, ALL), 1) >> 1) & 3) == m
    diag = row_sum(jnp.where(left == right, logits, 0.0))
    loss = jnp.sum(
        jnp.where(rows_m, 0.5 * jnp.log(row_total) - diag, 0.0), axis=0, keepdims=True
    ) + row_sum(jnp.where(cols_m, 0.5 * jnp.log(col_total), 0.0))
    loss_ref[...] = jnp.broadcast_to(loss * (1.0 / PAIRS), (8, 128))
    d_unit = LOGIT_SCALE * dot_tn(grad.astype(BF16), emb_b)
    unit_ref[...] = (d_unit - unit * row_sum(unit * d_unit)) * other_inv
    gother_ref[...] = own_rows(unit_ref[pl.ds(d * GROUP, GROUP), :])[0:IMGS].astype(BF16)

    def spread_q(k, carry):
        spread(qbd_ref, k, unblocks(g_a[pl.ds(k, 1), 32:72].astype(F32)))
        return carry

    dp_wait(2, g_a)
    lax.fori_loop(0, N_DP, spread_q, 0)

    tp_copy(0, s_sc, d_sc).wait_recv()
    tp_copy(1, s_kv, d_kv).wait_recv()
    weights = jnp.concatenate([s_sc[...], d_sc[...]], axis=0).astype(F32).T.astype(BF16)
    factors = jnp.concatenate([s_kv[...], d_kv[...]], axis=0)
    half = pl.ds(pl.multiple_of(t * HALF, 128), HALF)
    for c in range(PAD_ROWS // CHUNK):
        at = pl.ds(c * CHUNK, CHUNK)
        dn = dot(weights[c * CHUNK : (c + 1) * CHUNK], factors)
        mu, inv = mu_ref[at, :], inv_ref[at, :]
        xh = (x_ref[at, :].astype(F32) - mu) * inv
        mean_grad = row_sum(dn) * (1.0 / D)
        mean_cross = row_sum(dn * xh) * (1.0 / D)
        dn_ref[...] = dn
        if c == 0:
            dn0_ref[...] = dn[0:8]
        xh = (x_ref[at, half].astype(F32) - mu) * inv
        grad_x = inv * (dn_ref[:, half] - mean_grad - xh * mean_cross)
        gtok_ref[pl.ds(c * CHUNK // 2, CHUNK // 2)] = grad_x.reshape(CHUNK // 2, IMGS, HALF).astype(
            BF16
        )

    all_wait(1, d_cg)
    extra = own_rows(
        jnp.concatenate([d_cg[p] + d_cg[p + N_MOD] for p in range(N_MOD)], axis=1)
    )
    dn = dn0_ref[...] + extra
    mu, inv = mu_ref[0:8, :], inv_ref[0:8, :]
    xh = (x_ref[0:16, :].astype(F32)[0:8] - mu) * inv
    mean_grad = row_sum(dn) * (1.0 / D)
    mean_cross = row_sum(dn * xh) * (1.0 / D)
    dn0_ref[...] = inv * (dn - mean_grad - xh * mean_cross) + own_rows(d_hidden)
    gtok_ref[0] = dn0_ref[:, half][0:IMGS].astype(BF16)

    def spread_c(k, carry):
        spread(dbd_ref, k, unblocks(g_b[pl.ds(k, 1), 16:56].astype(F32)))
        return carry

    dp_wait(3, g_b)
    lax.fori_loop(0, N_DP, spread_c, 0)
    gqkv_ref[2] = head_grad(g_a[:, 0:16], dbd_ref)
    early = g_a[...].astype(F32)
    late = g_b[...].astype(F32)
    dhid_all = unblocks(late[:, 0:8]).astype(BF16)
    gout_ref[...] = dot_tn(dhid_all, unblocks(early[:, 72:112]).astype(BF16))[0:OUT_ROWS]
    pinv_all = unblocks(late[:, 8:16])
    pinv_all = pinv_all[:, 0:1] + pinv_all[:, 64:65]
    emb = emb_b.astype(F32)
    d_embed = LOGIT_SCALE * dot(grad.astype(BF16), unit_b)
    d_proj = (d_embed - emb * row_sum(emb * d_embed)) * pinv_all
    hn_all = unblocks(early[:, 24:32]).astype(BF16)
    gproj_ref[...] = dot_tn(hn_all, d_proj.astype(BF16))[0:OUT_ROWS]
    n0_all = unblocks(early[:, 16:24]).astype(BF16)
    for wait in leaving[:-2]:
        wait()
    del leaving[:-2]
    dp_wait(4, g_c)
    gqkv_ref[1] = head_grad(g_c[:, 0:16], qbd_ref)
    dq_all = unblocks(g_c[...].astype(F32)[:, 16:56]).astype(BF16)
    gqkv_ref[0] = dot_tn(n0_all, dq_all)[0:OUT_ROWS]

    for wait in leaving:
        wait()


def store(*refs):
    sources, targets, sem = refs[:6], refs[6:12], refs[12]
    copies = [
        pltpu.make_async_copy(src, dst, sem.at[k])
        for k, (src, dst) in enumerate(
            [(sources[1].at[pl.ds(0, TOK)], targets[1])] + list(zip(sources[2:], targets[2:]))
        )
    ]
    for copy in copies:
        copy.start()
    targets[0][0] = jnp.max(sources[0][0:1, 0:1])
    for copy in copies:
        copy.wait()


def local(tokens, w_qkv, w_out, w_proj, other_emb):
    vmem = pl.BlockSpec(memory_space=pltpu.VMEM)
    hbm = pl.BlockSpec(memory_space=pltpu.HBM)

    def pair(send, land, dtype=F32):
        return [pltpu.VMEM(send, dtype), pltpu.VMEM(land, dtype)]

    def mod_all(n, k):
        return pair((n, k), (N_MOD, n, k))

    def mod_each(n):
        return pair((N_MOD, n, SLICE), (N_MOD, n, SLICE), BF16)

    def dp_all(n):
        return pair((n, 128), (N_DP, n, 128), BF16)

    def dp_each(n):
        return pair((N_DP, n, 128), (N_DP, n, 128), BF16)

    scratch = [pltpu.VMEM((IMGS, E), BF16), pltpu.VMEM((TOK, IMGS, D), BF16), pltpu.VMEM((PAD_ROWS, D), BF16)]
    scratch += [pltpu.VMEM((PAD_ROWS, HALF), BF16)]
    scratch += [pltpu.VMEM((SLICE, HALF), BF16)]
    scratch += [pltpu.VMEM((N_MOD, SLICE, k), BF16) for k in COLUMNS]
    scratch += [
        pltpu.VMEM((PAD_ROWS, D), BF16),
        pltpu.VMEM((PAD_ROWS, 1), F32),
        pltpu.VMEM((PAD_ROWS, 1), F32),
        pltpu.VMEM((ALL, ALL), F32),
        pltpu.VMEM((CHUNK, D), F32),
        pltpu.VMEM((8, D), F32),
        pltpu.VMEM((ALL, E), F32),
        pltpu.VMEM((4, N_DP * 16, HALF), BF16),
        pltpu.VMEM((4, N_DP * 16, HALF), BF16),
        pltpu.VMEM((N_MOD, GROUP, SLICE), F32),
        pltpu.VMEM((N_MOD, GROUP, SLICE), F32),
    ]
    scratch += mod_each(16) + pair((64, 128), (N_MOD, 64, 128), BF16) + mod_all(8, HALF) + mod_each(16) + mod_each(16)
    scratch += mod_all(8, HALF) + pair((8, SLICE), (2 * N_MOD, 8, SLICE))
    scratch += mod_each(32) + pair((8, SLICE), (2 * N_MOD, 8, SLICE))
    scratch += pair((32, PAD_ROWS), (32, PAD_ROWS), BF16) + pair((32, D), (32, D), BF16)
    scratch += dp_all(64) + dp_all(64) + dp_each(112) + dp_each(64) + dp_each(64)
    dma = pltpu.SemaphoreType.DMA
    n = len(COLUMNS)
    scratch += [dma((n + 3,)), dma, dma((n,)), dma, dma((n,))]
    scratch += [dma((n,)), dma((n,)), dma((n,)), dma((n, 2))]
    scratch += [dma((7,)), dma((7,)), dma((2,)), dma((2,)), dma((2,)), dma((2,))]
    scratch += [dma((5,)), dma((5,))]

    def shape(*dims, dtype=F32):
        return jax.ShapeDtypeStruct(dims, dtype)

    results = pl.pallas_call(
        kernel,
        out_shape=[
            shape(8, 128),
            shape(PAD_TOK, IMGS, HALF, dtype=BF16),
            shape(3, OUT_ROWS, HALF),
            shape(OUT_ROWS, HALF),
            shape(OUT_ROWS, E),
            shape(IMGS, E, dtype=BF16),
        ],
        in_specs=[hbm] * 5,
        out_specs=[vmem] * 6,
        scratch_shapes=scratch,
        compiler_params=pltpu.CompilerParams(
            collective_id=0, has_side_effects=True, vmem_limit_bytes=48 * 2**20
        ),
    )(
        *(
            pltpu.with_memory_space_constraint(v, pltpu.HBM)
            for v in (
                tokens.transpose(1, 0, 2), w_qkv.transpose(1, 0, 2), w_out, w_proj, other_emb
            )
        )
    )
    loss, grad_tokens, grad_qkv, grad_out, grad_proj, grad_other = pl.pallas_call(
        store,
        out_shape=[
            shape(1),
            shape(TOK, IMGS, HALF, dtype=BF16),
            shape(3, OUT_ROWS, HALF),
            shape(OUT_ROWS, HALF),
            shape(OUT_ROWS, E),
            shape(IMGS, E, dtype=BF16),
        ],
        in_specs=[vmem] * 6,
        out_specs=[pl.BlockSpec(memory_space=pltpu.SMEM)] + [hbm] * 5,
        scratch_shapes=[pltpu.SemaphoreType.DMA((5,))],
        compiler_params=pltpu.CompilerParams(vmem_limit_bytes=16 * 2**20),
    )(*results)
    return (
        loss,
        grad_tokens.transpose(1, 0, 2),
        grad_qkv.transpose(1, 0, 2),
        grad_out,
        grad_proj,
        grad_other,
    )


def solution(mesh):
    placed = (
        P(("mod", "dp"), None, None),
        P("mod", None, "tp"),
        P("mod", "tp"),
        P("mod", None),
        P(("mod", "dp"), None),
    )
    return jax.shard_map(
        local,
        mesh=mesh,
        in_specs=placed,
        out_specs=(
            P("mod"),
            P(("mod", "dp"), None, "tp"),
            P(("mod", "dp"), None, "tp"),
            P(("mod", "dp"), "tp"),
            P(("mod", "dp"), None),
            P(("mod", "dp"), None),
        ),
        check_vma=False,
    )
```
